32 devices in a mesh: rep: 2 (over y), tp: 8 (over z, x), dp: 2 (over core).
Axes of the slice: x: 2, y: 2, z: 4, core: 2. Of those that a mesh axis runs over, the one named last changes fastest.
Arguments:
- tokens: bfloat16 [4096, 8192], P(('rep', 'dp'), 'tp'), parts along dimension 0, may hold values from -6 to 6
- query_weight: bfloat16 [8192, 8192], P('dp', 'tp'), may hold values from -0.0625 to 0.0625
- shrink_factors: bfloat16 [8192, 2048], P(None, ('rep', 'tp')), parts along dimension 1, may hold values from -0.0625 to 0.0625
- expand_factors: bfloat16 [2048, 8192], P(('rep', 'tp')), parts along dimension 0, may hold values from -1.5 to 1.5
- row_adapter_index: int32 [4096, 1], P(('rep', 'dp')), parts along dimension 0, may hold values from 0 to 63, as said below
- adapter_storage_block: int32 [128], P('rep'), parts along dimension 0, may hold values from 0 to 63, as said below
Outputs:
- query: bfloat16 [4096, 8192], P(('rep', 'dp'), 'tp'), parts along dimension 0
The draws below stay inside these ranges and needn't reach their ends.
There are 2 independent parts, one for each index of `rep`. The reference program is written for one: setup_inputs(seed, part) draws one part's arguments, and reference() takes and returns one part's arrays. A program takes and returns all parts, laid end to end along the dimension named above; an argument that names none is the same for every part. Nothing has to cross between parts.
Inputs may be any that keep to these rules, and one draw needn't show every extreme that they name: adapter_storage_block is a permutation of 0 to 63; storage block p lies on tp index p // 8. `row_adapter_index`: in each aligned block of 1024 rows, at most 256 rows use adapters whose storage blocks lie on one tp index, and in every block some tp index has exactly 256 such rows.
All inputs are finite; a program needn't handle non-finite values.
Results may differ from the reference program's by a relative error of at most 0.0051.
Values may be sent and summed in bfloat16 or wider, within the bound.
No kernel may reach another device: no remote copies, remote signals or barrier semaphores. Data moves between devices by JAX's collectives and lax.ppermute only.
A program may use at most 192 MiB of HBM per device.

```python
import jax
import jax.numpy as jnp
from jax import lax

MODEL_WIDTH = 8192
ADAPTER_RANK = 16
ADP_DEV = 8
TOK_DEV = 1024
ADAPTER_COUNT = 64
GROUP_TOKENS = 2048
CAP = 256


def adapter_order(key):
    return jax.random.permutation(key, ADAPTER_COUNT).astype(jnp.int32)


def draw_adapter_storage_block(key, part):
    storage = adapter_order(key)
    return storage


def one_block(key, inverse):
    holder_count = ADAPTER_COUNT // ADP_DEV
    slot_count = holder_count * CAP
    key_hot, key_rank, key_order, key_local = jax.random.split(key, 4)
    hot_owner = jax.random.randint(key_hot, (), 0, holder_count)
    rankings = jax.random.permutation(key_rank, slot_count).astype(jnp.int32)
    slot_owner = jnp.arange(slot_count, dtype=jnp.int32) // CAP
    scores = rankings + jnp.where(slot_owner == hot_owner, slot_count, 0)
    ordering = jnp.argsort(-scores, stable=True)
    chosen = ordering[:TOK_DEV]
    chosen = chosen[jax.random.permutation(key_order, TOK_DEV)]
    local_slot = jax.random.randint(key_local, (TOK_DEV,), 0, ADP_DEV)
    storage_weights = chosen // CAP * ADP_DEV + local_slot
    return jnp.take(inverse, storage_weights)


def draw_row_adapter_index(key, part):
    storage = adapter_order(key)
    key = jax.random.fold_in(key, 2)
    inverse = jnp.argsort(storage, stable=True).astype(jnp.int32)
    block_keys = jax.random.split(key, GROUP_TOKENS // TOK_DEV)
    adapter_rows = jax.vmap(one_block, in_axes=(0, None))(block_keys, inverse)
    return adapter_rows.reshape(GROUP_TOKENS, 1).astype(jnp.int32)


def level_of(own_key, dims, cuts, low, largest):
    def one(axis_at, shards_of):
        draws = jax.random.uniform(jax.random.fold_in(jax.random.fold_in(own_key, 6), axis_at), (shards_of,), jnp.float32, low / len(cuts), largest / len(cuts))
        return jnp.repeat(jnp.exp(draws), dims[axis_at] // shards_of).reshape((-1,) + (1,) * (len(dims) - axis_at - 1))

    level = one(*cuts[0])
    for cut in cuts[1:]:
        level = level * one(*cut)
    return level


def centred(own_key, shape, spread, limit, pieces=(), kind=jnp.bfloat16):
    array = spread * jax.random.normal(own_key, shape, jnp.float32)
    if pieces:
        array = array * level_of(own_key, shape, pieces, -0.22, 0.18)
    return jnp.clip(array, -limit, limit).astype(kind)


def setup_inputs(seed: int = 0, part: int = 0) -> dict:
    arg_keys = jax.random.split(jax.random.key(seed), 7)
    own_keys = jax.random.split(jax.random.fold_in(arg_keys[6], part), 7)
    return {
        "tokens": centred(own_keys[0], (GROUP_TOKENS, MODEL_WIDTH), 1.0, 6.0, ((0, 2), (1, 8))),
        "query_weight": centred(arg_keys[1], (MODEL_WIDTH, MODEL_WIDTH), MODEL_WIDTH ** -0.5, 0.0625, ((0, 2), (1, 8))),
        "shrink_factors": centred(own_keys[2], (MODEL_WIDTH, ADAPTER_COUNT * ADAPTER_RANK), MODEL_WIDTH ** -0.5, 0.0625, ((1, 8),)),
        "expand_factors": centred(own_keys[3], (ADAPTER_COUNT * ADAPTER_RANK, MODEL_WIDTH), ADAPTER_RANK ** -0.5, 1.5, ((0, 8),)),
        "row_adapter_index": draw_row_adapter_index(jax.random.fold_in(jax.random.fold_in(arg_keys[6], part), 71), part),
        "adapter_storage_block": draw_adapter_storage_block(jax.random.fold_in(jax.random.fold_in(arg_keys[6], part), 71), part),
    }


def reference(tokens, query_weight, shrink_factors, expand_factors, row_adapter_index, adapter_storage_block):
    base_output = jnp.dot(tokens, query_weight, preferred_element_type=jnp.float32)
    storage_weights = jnp.take(adapter_storage_block, row_adapter_index[:, 0]).astype(jnp.int32)
    shrink_weight_table = shrink_factors.reshape(MODEL_WIDTH, ADAPTER_COUNT, ADAPTER_RANK)
    expand_weight_table = expand_factors.reshape(ADAPTER_COUNT, ADAPTER_RANK, MODEL_WIDTH)

    def adapter_block_fn(operand):
        row_block, stored_block = operand
        shrink_rows = jnp.take(shrink_weight_table, stored_block, axis=1).astype(jnp.float32)
        reduced_rows = jnp.einsum("td,dtr->tr", row_block.astype(jnp.float32), shrink_rows).astype(jnp.bfloat16)
        reduced_rows = lax.optimization_barrier(reduced_rows)
        expand_rows = jnp.take(expand_weight_table, stored_block, axis=0).astype(jnp.float32)
        return jnp.einsum("tr,trd->td", reduced_rows.astype(jnp.float32), expand_rows).astype(jnp.bfloat16)

    adapter_output = lax.map(adapter_block_fn, (tokens.reshape(-1, 128, MODEL_WIDTH), storage_weights.reshape(-1, 128)))
    adapter_output = lax.optimization_barrier(adapter_output.reshape(GROUP_TOKENS, MODEL_WIDTH))
    return (base_output + adapter_output.astype(jnp.float32)).astype(jnp.bfloat16)
```

```python
import jax
import jax.numpy as jnp
from jax import lax
from jax.sharding import PartitionSpec as P

ADAPTER_RANK = 16
ROW_CHUNKS = (256, 256, 256, 256)


def general_body(
    tokens, query_weight, shrink_factors, expand_factors, row_adapter_index, adapter_storage_block
):
    holder_count = lax.axis_size("tp")
    own_index = lax.axis_index("tp")
    rows_per_holder = shrink_factors.shape[1] // ADAPTER_RANK
    row_count = tokens.shape[0]
    capacity = 2 * row_count // holder_count
    full_rows = lax.all_gather(tokens, "tp", axis=1, tiled=True)
    weight = lax.all_gather(query_weight, "dp", axis=0, tiled=True)
    base_output = jnp.dot(full_rows, weight, preferred_element_type=jnp.float32)
    storage_weights = jnp.take(adapter_storage_block, row_adapter_index[:, 0])
    owner_of = storage_weights // rows_per_holder
    local_of = storage_weights % rows_per_holder
    onehot = (owner_of[:, None] == jnp.arange(holder_count)[None, :]).astype(jnp.int32)
    rank_in_owner = jnp.sum(jnp.cumsum(onehot, axis=0) * onehot, axis=1) - 1
    select = (owner_of[None, :] == own_index) & (
        rank_in_owner[None, :] == jnp.arange(capacity)[:, None]
    )
    selected_rows = jnp.dot(
        select.astype(jnp.bfloat16), full_rows, preferred_element_type=jnp.float32
    ).astype(jnp.bfloat16)
    picked_local = jnp.sum(select.astype(jnp.int32) * local_of[None, :], axis=1)
    reduced_rows = jnp.dot(selected_rows, shrink_factors, preferred_element_type=jnp.float32)
    column_block = jnp.arange(rows_per_holder * ADAPTER_RANK) // ADAPTER_RANK
    keep_mask = column_block[None, :] == picked_local[:, None]
    masked = jnp.where(keep_mask, reduced_rows, 0.0)
    compact = jnp.sum(masked.reshape(capacity, rows_per_holder, ADAPTER_RANK), axis=1)
    spread = jnp.dot(select.T.astype(jnp.float32), compact, precision=lax.Precision.HIGHEST)
    shrink_all = lax.psum(spread, "tp").astype(jnp.bfloat16)
    columns = lax.all_to_all(
        expand_factors.reshape(rows_per_holder * ADAPTER_RANK, holder_count, -1),
        "tp",
        split_axis=1,
        concat_axis=0,
        tiled=True,
    )
    columns = columns.reshape(holder_count * rows_per_holder, ADAPTER_RANK, -1)
    factor_rows = jnp.take(columns, storage_weights, axis=0)
    adapter_output = jnp.einsum(
        "tr,trc->tc", shrink_all, factor_rows, preferred_element_type=jnp.float32
    ).astype(jnp.bfloat16)
    adapter_output = lax.optimization_barrier(adapter_output)
    return (base_output + adapter_output.astype(jnp.float32)).astype(jnp.bfloat16)


def dot(a, b):
    return jnp.dot(a, b, preferred_element_type=jnp.float32)


def pick(a, j):
    return lax.dynamic_index_in_dim(a, j, 0, keepdims=False)


def line_body(
    tokens, query_weight, shrink_factors, expand_factors, row_adapter_index, adapter_storage_block
):
    tp = lax.axis_size("tp")
    planes = tp // 2
    own = lax.axis_index("tp")
    z, x = own // 2, own % 2
    r, d = lax.axis_index("rep"), lax.axis_index("dp")
    rows, depth = tokens.shape
    width = query_weight.shape[1]
    holder_columns = shrink_factors.shape[1]
    holder_adapters = holder_columns // ADAPTER_RANK
    half = holder_columns // 2
    across = [(i, i ^ 1) for i in range(tp)]
    swap = [(0, 1), (1, 0)]

    def up(h):
        return [(i, i + 2) for i in range(2 * (h - 1), tp - 2)]

    def down(h):
        return [(i + 2, i) for i in range(0, tp - 2 * h)]

    def place(plane):
        return 2 * ((plane // 2) ^ d) + ((plane % 2) ^ r)

    def plane_at(p):
        return 2 * ((p // 2) ^ d) + ((p % 2) ^ r)

    blocks = query_weight.reshape(planes, depth, width)
    outgoing = pick(blocks, 2 * r + (1 - x))
    near, far = [], []
    for part in jnp.split(outgoing, 2):
        got = lax.ppermute(part, "tp", across)
        near.append(got)
        far.append(lax.ppermute(got, "rep", swap))
    own_half = jnp.concatenate([pick(blocks, 2 * r + x), pick(blocks, 2 * (1 - r) + x)])
    other_half = jnp.concatenate(near + far)
    weight_own = jnp.concatenate([own_half, lax.ppermute(own_half, "dp", swap)])
    weight_other = jnp.concatenate([other_half, lax.ppermute(other_half, "dp", swap)])

    factors = shrink_factors.reshape(planes, 2, depth, holder_columns)
    shrink_own = jnp.concatenate([pick(pick(factors, plane_at(p)), x) for p in range(planes)])
    leaving = jnp.concatenate([pick(pick(factors, plane_at(p)), 1 - x) for p in range(planes // 2)])
    shrink_near = lax.ppermute(leaving, "tp", across)
    shrink_other = jnp.concatenate([shrink_near, lax.ppermute(shrink_near, "dp", swap)])
    shrink = jnp.concatenate([shrink_own, shrink_other], axis=1)

    expand_half = lax.dynamic_slice_in_dim(expand_factors, d * half, half, 0)
    expand_half = expand_half.reshape(half, tp, width).transpose(1, 0, 2)
    expand_half = lax.all_to_all(expand_half, "tp", split_axis=0, concat_axis=0, tiled=True)
    expand_half = expand_half.reshape(tp * half, width)
    expand = jnp.concatenate([expand_half, lax.ppermute(expand_half, "dp", swap)])

    known = jnp.arange(adapter_storage_block.shape[0])
    stored = jnp.sum(
        jnp.where(row_adapter_index == known[None, :], adapter_storage_block[None, :], 0),
        axis=1,
        keepdims=True,
    )
    column = jnp.arange(2 * holder_columns)
    column_adapter = (own ^ (column // holder_columns)) * holder_adapters + (
        column % holder_columns
    ) // ADAPTER_RANK
    fold = (column[:, None] % ADAPTER_RANK == jnp.arange(ADAPTER_RANK)[None, :]).astype(jnp.bfloat16)
    entry = jnp.arange(tp * holder_columns)
    within = entry % (tp * half)
    entry_adapter = (within // half) * holder_adapters + (
        ((entry // (tp * half)) ^ d) * half + within % half
    ) // ADAPTER_RANK
    unfold = (jnp.arange(ADAPTER_RANK)[:, None] == entry[None, :] % ADAPTER_RANK).astype(jnp.bfloat16)

    def lora(parts, first, count):
        shrunk = jnp.concatenate(parts)
        everyone = jnp.broadcast_to(shrunk[None], (tp,) + shrunk.shape)
        everyone = lax.all_to_all(everyone, "tp", split_axis=0, concat_axis=0, tiled=True)
        total = jnp.sum(everyone.astype(jnp.float32), axis=0).astype(jnp.bfloat16)
        spread = dot(total, unfold)
        mine = stored[first : first + count] == entry_adapter[None, :]
        return jnp.where(mine, spread, 0.0).astype(jnp.bfloat16)

    chunks = []
    first = 0
    gates = []
    for number, count in enumerate(ROW_CHUNKS):
        piece = tokens[first : first + count]
        if number >= 2:
            piece, _ = lax.optimization_barrier((piece, gates[number - 2]))
        upward, downward = {0: piece}, {0: piece}
        for h in range(1, planes):
            upward[h] = lax.ppermute(upward[h - 1], "tp", up(h))
            downward[h] = lax.ppermute(downward[h - 1], "tp", down(h))
        gates.append(downward[2])
        line = jnp.zeros((count, planes * depth), tokens.dtype)
        line = lax.dynamic_update_slice(line, piece, (0, place(z) * depth))
        for j in range(1, planes):
            block = jnp.where(z + j < planes, downward[j], upward[planes - j])
            line = lax.dynamic_update_slice(line, block, (0, place((z + j) % planes) * depth))
        partial = dot(line, weight_other).astype(jnp.bfloat16)
        partial = lax.ppermute(partial, "tp", across)
        reduced = dot(line, shrink)
        mine = stored[first : first + count] == column_adapter[None, :]
        shrunk = dot(jnp.where(mine, reduced, 0.0).astype(jnp.bfloat16), fold).astype(jnp.bfloat16)
        base = dot(line, weight_own)
        chunks.append((first, count, base, partial, shrunk))
        first += count

    outs = []
    for group in (chunks[:-1], chunks[-1:]):
        start = group[0][0]
        size = sum(c[1] for c in group)
        spread = lora([c[4] for c in group], start, size)
        for first, count, base, partial, _ in group:
            added = dot(spread[first - start : first - start + count], expand)
            outs.append((base + partial.astype(jnp.float32) + added).astype(jnp.bfloat16))
    return jnp.concatenate(outs)


def solution(mesh):
    placed = (
        P(("rep", "dp"), "tp"),
        P("dp", "tp"),
        P(None, ("rep", "tp")),
        P(("rep", "tp"), None),
        P(("rep", "dp"), None),
        P("rep"),
    )
    lined = dict(mesh.shape) == {"rep": 2, "tp": 8, "dp": 2}
    return jax.shard_map(
        line_body if lined else general_body,
        mesh=mesh,
        in_specs=placed,
        out_specs=P(("rep", "dp"), "tp"),
        check_vma=False,
    )
```

```python
import jax
import jax.numpy as jnp
from jax import lax
from jax.experimental import pallas as pl
from jax.experimental.pallas import tpu as pltpu
from jax.sharding import PartitionSpec as P

ADAPTER_RANK = 16
ROW_CHUNKS = (640, 384)
ROW_STEP = 128
SOURCES = 6
VMEM_BYTES = 56 * 1024 * 1024


def general_body(
    tokens, query_weight, shrink_factors, expand_factors, row_adapter_index, adapter_storage_block
):
    holder_count = lax.axis_size("tp")
    own_index = lax.axis_index("tp")
    rows_per_holder = shrink_factors.shape[1] // ADAPTER_RANK
    row_count = tokens.shape[0]
    capacity = 2 * row_count // holder_count
    full_rows = lax.all_gather(tokens, "tp", axis=1, tiled=True)
    weight = lax.all_gather(query_weight, "dp", axis=0, tiled=True)
    base_output = jnp.dot(full_rows, weight, preferred_element_type=jnp.float32)
    storage_weights = jnp.take(adapter_storage_block, row_adapter_index[:, 0])
    owner_of = storage_weights // rows_per_holder
    local_of = storage_weights % rows_per_holder
    onehot = (owner_of[:, None] == jnp.arange(holder_count)[None, :]).astype(jnp.int32)
    rank_in_owner = jnp.sum(jnp.cumsum(onehot, axis=0) * onehot, axis=1) - 1
    select = (owner_of[None, :] == own_index) & (
        rank_in_owner[None, :] == jnp.arange(capacity)[:, None]
    )
    selected_rows = jnp.dot(
        select.astype(jnp.bfloat16), full_rows, preferred_element_type=jnp.float32
    ).astype(jnp.bfloat16)
    picked_local = jnp.sum(select.astype(jnp.int32) * local_of[None, :], axis=1)
    reduced_rows = jnp.dot(selected_rows, shrink_factors, preferred_element_type=jnp.float32)
    column_block = jnp.arange(rows_per_holder * ADAPTER_RANK) // ADAPTER_RANK
    keep_mask = column_block[None, :] == picked_local[:, None]
    masked = jnp.where(keep_mask, reduced_rows, 0.0)
    compact = jnp.sum(masked.reshape(capacity, rows_per_holder, ADAPTER_RANK), axis=1)
    spread = jnp.dot(select.T.astype(jnp.float32), compact, precision=lax.Precision.HIGHEST)
    shrink_all = lax.psum(spread, "tp").astype(jnp.bfloat16)
    columns = lax.all_to_all(
        expand_factors.reshape(rows_per_holder * ADAPTER_RANK, holder_count, -1),
        "tp",
        split_axis=1,
        concat_axis=0,
        tiled=True,
    )
    columns = columns.reshape(holder_count * rows_per_holder, ADAPTER_RANK, -1)
    factor_rows = jnp.take(columns, storage_weights, axis=0)
    adapter_output = jnp.einsum(
        "tr,trc->tc", shrink_all, factor_rows, preferred_element_type=jnp.float32
    ).astype(jnp.bfloat16)
    adapter_output = lax.optimization_barrier(adapter_output)
    return (base_output + adapter_output.astype(jnp.float32)).astype(jnp.bfloat16)


def dot(a, b):
    return jnp.dot(a, b, preferred_element_type=jnp.float32)


def pick(a, j):
    return lax.dynamic_index_in_dim(a, j, 0, keepdims=False)


def early_kernel(sel, place, *refs):
    sources, refs = refs[: SOURCES - 1], refs[SOURCES - 1 :]
    pieces, refs = refs[:4], refs[4:]
    factors, (total, line, weight, sems) = refs[:3], refs[3:]
    depth, width = pieces[0].shape
    columns, half = factors[0].shape[1], factors[1].shape[0]
    steps = sel.shape[0]

    def arrive(j, source, piece, tail):
        own_rows = pl.ds(pl.multiple_of(place[j] * depth, depth), depth)
        tail_rows = pl.ds(pl.multiple_of(lax.rem(place[j], 2) * depth, depth), depth)
        return [
            pltpu.make_async_copy(source, line.at[j], sems.at[j, 0]),
            pltpu.make_async_copy(piece, weight.at[j, :, pl.ds(0, width)], sems.at[j, 1]),
            pltpu.make_async_copy(
                factors[0].at[own_rows], weight.at[j, :, pl.ds(width, columns)], sems.at[j, 2]
            ),
            pltpu.make_async_copy(
                tail.at[tail_rows], weight.at[j, :, pl.ds(width + columns, columns)], sems.at[j, 3]
            ),
        ]

    for j in range(steps):
        for number, source in enumerate(sources):

            @pl.when(sel[j] == number)
            def _():
                arrive(j, source, pieces[0], factors[1])[0].start()

        for number, piece in enumerate(pieces):

            @pl.when((place[j] == number) & (sel[j] < SOURCES - 1))
            def _():
                for copy in arrive(j, sources[0], piece, factors[1 + number // 2])[1:]:
                    copy.start()

    for j in range(steps):

        @pl.when(sel[j] < SOURCES - 1)
        def _():
            for copy in arrive(j, sources[0], pieces[0], factors[1]):
                copy.wait()
            term = dot(line[j], weight[j])
            if j == 0:
                total[...] = term
            else:
                total[...] += term


def rest_kernel(farthest, total, block, *refs):
    pieces, refs = refs[:4], refs[4:]
    factors, refs = refs[:3], refs[3:]
    stored, adapter, fold, partial, shrunk, weight, sems = refs
    depth, width = pieces[0].shape
    columns = factors[0].shape[1]
    own_rows = pl.ds(pl.multiple_of(farthest[0] * depth, depth), depth)
    tail_rows = pl.ds(pl.multiple_of(lax.rem(farthest[0], 2) * depth, depth), depth)

    def arrive(piece, tail):
        return [
            pltpu.make_async_copy(piece, weight.at[:, pl.ds(0, width)], sems.at[0]),
            pltpu.make_async_copy(
                factors[0].at[own_rows], weight.at[:, pl.ds(width, columns)], sems.at[1]
            ),
            pltpu.make_async_copy(
                tail.at[tail_rows], weight.at[:, pl.ds(width + columns, columns)], sems.at[2]
            ),
        ]

    for number, piece in enumerate(pieces):

        @pl.when(farthest[0] == number)
        def _():
            for copy in arrive(piece, factors[1 + number // 2]):
                copy.start()

    for copy in arrive(pieces[0], factors[1]):
        copy.wait()
    full = total[...] + dot(block[...], weight[...])
    partial[...] = full[:, :width].astype(partial.dtype)
    kept = jnp.where(stored[...] == adapter[...], full[:, width:], 0.0).astype(jnp.bfloat16)
    across = (((1,), (1,)), ((), ()))
    shrunk[...] = lax.dot_general(
        fold[...], kept, across, preferred_element_type=jnp.float32
    ).astype(shrunk.dtype)


def own_kernel(sel, place, *refs):
    sources, refs = refs[: SOURCES - 1], refs[SOURCES - 1 :]
    halves, (base, line, weight, sems) = refs[:2], refs[2:]
    depth = sources[0].shape[1]
    steps = sel.shape[0]

    def copies(j, source, half):
        rows = pl.ds(pl.multiple_of(lax.rem(place[j], 2) * depth, depth), depth)
        return [
            pltpu.make_async_copy(source, line.at[j], sems.at[j, 0]),
            pltpu.make_async_copy(half.at[rows], weight.at[j], sems.at[j, 1]),
        ]

    for j in range(steps):
        for number, source in enumerate(sources):

            @pl.when(sel[j] == number)
            def _():
                copies(j, source, halves[0])[0].start()

        for number, half in enumerate(halves):

            @pl.when((place[j] // 2 == number) & (sel[j] < SOURCES - 1))
            def _():
                copies(j, sources[0], half)[1].start()

    for j in range(steps):

        @pl.when(sel[j] < SOURCES - 1)
        def _():
            for copy in copies(j, sources[0], halves[0]):
                copy.wait()
            term = dot(line[j], weight[j])
            if j == 0:
                base[...] = term
            else:
                base[...] += term


def lora_kernel(farthest, base, everyone, stored, adapter, unfold, *refs):
    expand, block, weights, refs = refs[:2], refs[2], refs[3:5], refs[5:]
    partials, (out, weight, sem) = refs[:-3], refs[-3:]
    depth = weight.shape[0]
    rows = pl.ds(pl.multiple_of(farthest[0] * depth, depth), depth)
    for number, half in enumerate(weights):

        @pl.when(farthest[1] == number)
        def _():
            pltpu.make_async_copy(half.at[rows], weight, sem).start()

    shrunk = jnp.sum(everyone[...].astype(jnp.float32), axis=0).astype(jnp.bfloat16)
    spread = lax.dot_general(
        shrunk, unfold[...], (((0,), (0,)), ((), ())), preferred_element_type=jnp.float32
    )
    spread = jnp.where(stored[...] == adapter[...], spread, 0.0).astype(jnp.bfloat16)
    half = spread.shape[1] // 2
    added = dot(spread[:, :half], expand[0][...]) + dot(spread[:, half:], expand[1][...])
    pltpu.make_async_copy(weights[0].at[rows], weight, sem).wait()
    added = base[...] + added + dot(block[...], weight[...])
    for partial in partials:
        added += partial[...].astype(jnp.float32)
    out[...] = added.astype(out.dtype)


def sum_kernel(base, partial, *refs):
    refs[-1][...] = (base[...] + partial[...].astype(jnp.float32)).astype(jnp.bfloat16)


def whole(shape):
    return pl.BlockSpec(shape, lambda n, *_: (0,) * len(shape))


def on_line(kernel, scalars, sources, weights, small, outs, scratch):
    rows, depth = sources[0].shape
    planes = scalars[0].shape[0]
    width = weights[0].shape[-1]
    flops = 2 * rows * planes * depth * width
    size = 2 * planes * depth * width + 2 * rows * planes * depth + 4 * rows * width
    return pl.pallas_call(
        kernel,
        grid_spec=pltpu.PrefetchScalarGridSpec(
            num_scalar_prefetch=2,
            grid=(1,),
            in_specs=[pl.BlockSpec(memory_space=pl.ANY) for _ in sources + weights]
            + [whole(v.shape) for v in small],
            out_specs=[whole(o.shape) for o in outs],
            scratch_shapes=scratch + [pltpu.SemaphoreType.DMA((planes, 4))],
        ),
        out_shape=outs,
        compiler_params=pltpu.CompilerParams(vmem_limit_bytes=VMEM_BYTES),
        cost_estimate=pl.CostEstimate(flops=flops, bytes_accessed=size, transcendentals=0),
    )(*scalars, *sources, *weights, *small)


def after(value, *events):
    return lax.optimization_barrier((value,) + events)[0]


def line_body(
    tokens, query_weight, shrink_factors, expand_factors, row_adapter_index, adapter_storage_block
):
    tp = lax.axis_size("tp")
    planes = tp // 2
    own = lax.axis_index("tp")
    z, x = own // 2, own % 2
    r, d = lax.axis_index("rep"), lax.axis_index("dp")
    rows, depth = tokens.shape
    width = query_weight.shape[1]
    holder_columns = shrink_factors.shape[1]
    holder_adapters = holder_columns // ADAPTER_RANK
    half = holder_columns // 2
    across = [(i, i ^ 1) for i in range(tp)]
    swap = [(0, 1), (1, 0)]

    def up(h):
        return [(i, i + 2) for i in range(2 * (h - 1), tp - 2)]

    def down(h):
        return [(i + 2, i) for i in range(0, tp - 2 * h)]

    def place(plane):
        return 2 * ((plane // 2) ^ d) + ((plane % 2) ^ r)

    def plane_at(p):
        return 2 * ((p // 2) ^ d) + ((p % 2) ^ r)

    pieces, starts = [], []
    first = 0
    for count in ROW_CHUNKS:
        starts.append(first)
        pieces.append(tokens[first : first + count])
        first += count
    ups = [{0: p} for p in pieces]
    downs = [{0: p} for p in pieces]

    def hop(c, h):
        if h == planes - 1:
            inner = jnp.where(z == 1, downs[c][h - 1], ups[c][h - 1])
            pairs = [p for p in up(h) + down(h)]
            ups[c][h] = downs[c][h] = lax.ppermute(inner, "tp", pairs)
            return
        ups[c][h] = lax.ppermute(ups[c][h - 1], "tp", up(h))
        downs[c][h] = lax.ppermute(downs[c][h - 1], "tp", down(h))

    def step(values, *events):
        return lax.optimization_barrier((values, events))[0]

    def to_other_core(value):
        return lax.ppermute(value, "dp", swap)

    blocks = query_weight.reshape(planes, depth, width)
    hop(0, 1)
    hop(1, 1)
    near = lax.ppermute(pick(blocks, 2 * r + (1 - x)), "tp", across)

    factors = shrink_factors.reshape(planes, 2, depth, holder_columns)
    leaving = jnp.concatenate([pick(pick(factors, plane_at(p)), 1 - x) for p in range(planes // 2)])
    expand_half = lax.dynamic_slice_in_dim(expand_factors, d * half, half, 0)
    expand_half = expand_half.reshape(half, tp, width).transpose(1, 0, 2)
    (ups[0][1], downs[0][1], ups[1][1], downs[1][1], near, leaving, weights, factors, expand_half) = step(
        (ups[0][1], downs[0][1], ups[1][1], downs[1][1], near, leaving, query_weight, factors, expand_half)
    )
    hop(0, 2)
    far = lax.ppermute(near, "rep", swap)
    shrink_near = lax.ppermute(leaving, "tp", across)
    near_crossed = to_other_core(near)
    pairs = weights.reshape(planes // 2, 2, depth, width)
    own_half = lax.dynamic_index_in_dim(pairs, x, 1, keepdims=False).reshape(-1, width)
    shrink_own = jnp.concatenate([pick(pick(factors, plane_at(p)), x) for p in range(planes)])
    expand_half = lax.all_to_all(expand_half, "tp", split_axis=0, concat_axis=0, tiled=True)
    expand_half = expand_half.reshape(tp * half, width)

    (ups[0][2], downs[0][2], ups[1][1], downs[1][1], shrink_near, far, near_crossed, expand_half, own_half) = step(
        (ups[0][2], downs[0][2], ups[1][1], downs[1][1], shrink_near, far, near_crossed, expand_half, own_half)
    )
    hop(0, 3)
    shrink = [shrink_own, shrink_near, to_other_core(shrink_near)]
    weight_other = [near, far, near_crossed, to_other_core(far)]
    weight_own = [own_half, to_other_core(own_half)]

    known = jnp.arange(adapter_storage_block.shape[0])
    stored = jnp.sum(
        jnp.where(row_adapter_index == known[None, :], adapter_storage_block[None, :], 0),
        axis=1,
        keepdims=True,
    )
    column = jnp.arange(2 * holder_columns)
    column_adapter = (own ^ (column // holder_columns)) * holder_adapters + (
        column % holder_columns
    ) // ADAPTER_RANK
    column_adapter = column_adapter[None, :].astype(jnp.int32)
    fold = (jnp.arange(ADAPTER_RANK)[:, None] == column[None, :] % ADAPTER_RANK).astype(jnp.bfloat16)
    entry = jnp.arange(tp * holder_columns)
    within = entry % (tp * half)
    entry_adapter = (within // half) * holder_adapters + (
        ((entry // (tp * half)) ^ d) * half + within % half
    ) // ADAPTER_RANK
    entry_adapter = entry_adapter[None, :].astype(jnp.int32)
    unfold = (jnp.arange(ADAPTER_RANK)[:, None] == entry[None, :] % ADAPTER_RANK).astype(jnp.bfloat16)

    steps = jnp.arange(planes)
    above = z + steps < planes
    hops = jnp.where(above, steps, planes - steps)
    sel = jnp.where(
        steps == 0, 0, jnp.where(hops == planes - 1, SOURCES - 1, hops + jnp.where(above, planes - 2, 0))
    ).astype(jnp.int32)
    plane = (z + steps) % planes
    places_other = place(plane).astype(jnp.int32)
    places_own = (2 * ((plane // 2) ^ d) + plane % 2).astype(jnp.int32)
    distant = jnp.where(z == 0, planes - 1, 0)
    farthest_other = place(distant).astype(jnp.int32)[None]
    farthest_own = jnp.stack([distant % 2, (distant // 2) ^ d]).astype(jnp.int32)

    def sources(c):
        between = range(1, planes - 1)
        return [pieces[c]] + [ups[c][h] for h in between] + [downs[c][h] for h in between] + [
            ups[c].get(planes - 1)
        ]

    total_columns = width + 2 * holder_columns

    def early_part(c, *events):
        count = ROW_CHUNKS[c]
        return on_line(
            early_kernel,
            [after(sel, *events) if events else sel, places_other],
            sources(c)[:-1],
            weight_other + shrink,
            [],
            [jax.ShapeDtypeStruct((count, total_columns), jnp.float32)],
            [
                pltpu.VMEM((planes, count, depth), jnp.bfloat16),
                pltpu.VMEM((planes, depth, total_columns), jnp.bfloat16),
            ],
        )[0]

    def rest_part(c, total):
        count = ROW_CHUNKS[c]
        small = [stored[starts[c] : starts[c] + count], column_adapter, fold]
        outs = [
            jax.ShapeDtypeStruct((count, width), jnp.bfloat16),
            jax.ShapeDtypeStruct((ADAPTER_RANK, count), jnp.bfloat16),
        ]
        return pl.pallas_call(
            rest_kernel,
            grid_spec=pltpu.PrefetchScalarGridSpec(
                num_scalar_prefetch=1,
                grid=(1,),
                in_specs=[whole(total.shape), whole((count, depth))]
                + [pl.BlockSpec(memory_space=pl.ANY) for _ in range(7)]
                + [whole(v.shape) for v in small],
                out_specs=[whole(o.shape) for o in outs],
                scratch_shapes=[
                    pltpu.VMEM((depth, total_columns), jnp.bfloat16),
                    pltpu.SemaphoreType.DMA((3,)),
                ],
            ),
            out_shape=outs,
            compiler_params=pltpu.CompilerParams(vmem_limit_bytes=VMEM_BYTES),
            cost_estimate=pl.CostEstimate(
                flops=2 * count * depth * total_columns, bytes_accessed=4 * depth * width, transcendentals=0
            ),
        )(farthest_other, total, ups[c][planes - 1], *weight_other, *shrink, *small)

    def own_part(c, *events):
        count = ROW_CHUNKS[c]
        return on_line(
            own_kernel,
            [after(sel, *events) if events else sel, places_own],
            sources(c)[:-1],
            weight_own,
            [],
            [jax.ShapeDtypeStruct((count, width), jnp.float32)],
            [
                pltpu.VMEM((planes, count, depth), jnp.bfloat16),
                pltpu.VMEM((planes, depth, width), jnp.bfloat16),
            ],
        )[0]

    def spread_out(shrunk):
        everyone = jnp.broadcast_to(shrunk[None], (tp,) + shrunk.shape)
        return lax.all_to_all(everyone, "tp", split_axis=0, concat_axis=0, tiled=True)

    def lora_part(c, base, everyone, expand, partial=None):
        count = ROW_CHUNKS[c]
        rows_of = whole((count, width))
        partials = [] if partial is None else [partial]
        out = (count, width, jnp.float32) if partial is None else (rows, width, jnp.bfloat16)
        return pl.pallas_call(
            lora_kernel,
            grid_spec=pltpu.PrefetchScalarGridSpec(
                num_scalar_prefetch=1,
                grid=(1,),
                in_specs=[
                    rows_of,
                    whole(everyone.shape),
                    whole((count, 1)),
                    whole(entry_adapter.shape),
                    whole(unfold.shape),
                    whole(expand[0].shape),
                    whole(expand[1].shape),
                    whole((count, depth)),
                ]
                + [pl.BlockSpec(memory_space=pl.ANY)] * 2
                + [rows_of for _ in partials],
                out_specs=rows_of,
                scratch_shapes=[pltpu.VMEM((depth, width), jnp.bfloat16), pltpu.SemaphoreType.DMA],
            ),
            out_shape=jax.ShapeDtypeStruct(out[:2], out[2]),
            compiler_params=pltpu.CompilerParams(vmem_limit_bytes=VMEM_BYTES),
            cost_estimate=pl.CostEstimate(
                flops=4 * count * width * depth, bytes_accessed=4 * depth * width, transcendentals=0
            ),
        )(
            farthest_own,
            base,
            everyone,
            stored[starts[c] : starts[c] + count],
            entry_adapter,
            unfold,
            *expand,
            ups[c][planes - 1],
            *weight_own,
            *partials,
        )

    def sum_part(c, base, partial, earlier):
        count, step = ROW_CHUNKS[c], ROW_STEP
        here = starts[c] // step
        rows_of = pl.BlockSpec((step, width), lambda i: (i, 0))
        operands = [base, partial, earlier]
        specs = [rows_of, rows_of, pl.BlockSpec(memory_space=pl.ANY)]
        aliases = {2: 0}
        return pl.pallas_call(
            sum_kernel,
            grid=(count // step,),
            in_specs=specs,
            out_specs=pl.BlockSpec((step, width), lambda i: (i + here, 0)),
            out_shape=jax.ShapeDtypeStruct((rows, width), jnp.bfloat16),
            input_output_aliases=aliases,
            compiler_params=pltpu.CompilerParams(vmem_limit_bytes=VMEM_BYTES),
            cost_estimate=pl.CostEstimate(
                flops=2 * count * width, bytes_accessed=8 * count * width, transcendentals=0
            ),
        )(*operands)

    early_a = early_part(0)
    base_a = own_part(0, early_a)
    (ups[0][3], ups[1][1], downs[1][1], expand_half) = step(
        (ups[0][3], ups[1][1], downs[1][1], expand_half), base_a
    )
    hop(1, 2)
    expand = [expand_half, to_other_core(expand_half)]
    partial_a, shrunk_a = rest_part(0, early_a)
    got_a = lax.ppermute(partial_a, "tp", across)
    ups[1][2], downs[1][2] = step((ups[1][2], downs[1][2]), partial_a)
    hop(1, 3)
    everyone_a = spread_out(shrunk_a)
    early_c = early_part(1)
    base_c = own_part(1, early_c, everyone_a)
    ups[1][3] = step(ups[1][3], base_c, got_a)
    partial_c, shrunk_c = rest_part(1, early_c)
    got_c = lax.ppermute(partial_c, "tp", across)
    everyone_c = spread_out(shrunk_c)
    out = lora_part(0, base_a, everyone_a, expand, got_a)
    whole_c = lora_part(1, base_c, everyone_c, expand)
    return sum_part(1, whole_c, got_c, out)


def solution(mesh):
    placed = (
        P(("rep", "dp"), "tp"),
        P("dp", "tp"),
        P(None, ("rep", "tp")),
        P(("rep", "tp"), None),
        P(("rep", "dp"), None),
        P("rep"),
    )
    lined = dict(mesh.shape) == {"rep": 2, "tp": 8, "dp": 2}
    return jax.shard_map(
        line_body if lined else general_body,
        mesh=mesh,
        in_specs=placed,
        out_specs=P(("rep", "dp"), "tp"),
        check_vma=False,
    )
```

```python
import jax
import jax.numpy as jnp
from jax import lax
from jax.experimental import pallas as pl
from jax.experimental.pallas import tpu as pltpu
from jax.sharding import PartitionSpec as P

ADAPTER_RANK = 16
ROW_CHUNKS = (640, 384)
ROW_STEP = 128
SOURCES = 6
VMEM_BYTES = 56 * 1024 * 1024


def general_body(
    tokens, query_weight, shrink_factors, expand_factors, row_adapter_index, adapter_storage_block
):
    holder_count = lax.axis_size("tp")
    own_index = lax.axis_index("tp")
    rows_per_holder = shrink_factors.shape[1] // ADAPTER_RANK
    row_count = tokens.shape[0]
    capacity = 2 * row_count // holder_count
    full_rows = lax.all_gather(tokens, "tp", axis=1, tiled=True)
    weight = lax.all_gather(query_weight, "dp", axis=0, tiled=True)
    base_output = jnp.dot(full_rows, weight, preferred_element_type=jnp.float32)
    storage_weights = jnp.take(adapter_storage_block, row_adapter_index[:, 0])
    owner_of = storage_weights // rows_per_holder
    local_of = storage_weights % rows_per_holder
    onehot = (owner_of[:, None] == jnp.arange(holder_count)[None, :]).astype(jnp.int32)
    rank_in_owner = jnp.sum(jnp.cumsum(onehot, axis=0) * onehot, axis=1) - 1
    select = (owner_of[None, :] == own_index) & (
        rank_in_owner[None, :] == jnp.arange(capacity)[:, None]
    )
    selected_rows = jnp.dot(
        select.astype(jnp.bfloat16), full_rows, preferred_element_type=jnp.float32
    ).astype(jnp.bfloat16)
    picked_local = jnp.sum(select.astype(jnp.int32) * local_of[None, :], axis=1)
    reduced_rows = jnp.dot(selected_rows, shrink_factors, preferred_element_type=jnp.float32)
    column_block = jnp.arange(rows_per_holder * ADAPTER_RANK) // ADAPTER_RANK
    keep_mask = column_block[None, :] == picked_local[:, None]
    masked = jnp.where(keep_mask, reduced_rows, 0.0)
    compact = jnp.sum(masked.reshape(capacity, rows_per_holder, ADAPTER_RANK), axis=1)
    spread = jnp.dot(select.T.astype(jnp.float32), compact, precision=lax.Precision.HIGHEST)
    shrink_all = lax.psum(spread, "tp").astype(jnp.bfloat16)
    columns = lax.all_to_all(
        expand_factors.reshape(rows_per_holder * ADAPTER_RANK, holder_count, -1),
        "tp",
        split_axis=1,
        concat_axis=0,
        tiled=True,
    )
    columns = columns.reshape(holder_count * rows_per_holder, ADAPTER_RANK, -1)
    factor_rows = jnp.take(columns, storage_weights, axis=0)
    adapter_output = jnp.einsum(
        "tr,trc->tc", shrink_all, factor_rows, preferred_element_type=jnp.float32
    ).astype(jnp.bfloat16)
    adapter_output = lax.optimization_barrier(adapter_output)
    return (base_output + adapter_output.astype(jnp.float32)).astype(jnp.bfloat16)


def dot(a, b):
    return jnp.dot(a, b, preferred_element_type=jnp.float32)


def pick(a, j):
    return lax.dynamic_index_in_dim(a, j, 0, keepdims=False)


def early_kernel(sel, place, *refs):
    sources, refs = refs[: SOURCES - 1], refs[SOURCES - 1 :]
    pieces, refs = refs[:4], refs[4:]
    factors, (total, line, weight, sems) = refs[:3], refs[3:]
    depth, width = pieces[0].shape
    columns, half = factors[0].shape[1], factors[1].shape[0]
    steps = sel.shape[0]

    def arrive(j, source, piece, tail):
        own_rows = pl.ds(pl.multiple_of(place[j] * depth, depth), depth)
        tail_rows = pl.ds(pl.multiple_of(lax.rem(place[j], 2) * depth, depth), depth)
        return [
            pltpu.make_async_copy(source, line.at[j], sems.at[j, 0]),
            pltpu.make_async_copy(piece, weight.at[j, :, pl.ds(0, width)], sems.at[j, 1]),
            pltpu.make_async_copy(
                factors[0].at[own_rows], weight.at[j, :, pl.ds(width, columns)], sems.at[j, 2]
            ),
            pltpu.make_async_copy(
                tail.at[tail_rows], weight.at[j, :, pl.ds(width + columns, columns)], sems.at[j, 3]
            ),
        ]

    for j in range(steps):
        for number, source in enumerate(sources):

            @pl.when(sel[j] == number)
            def _():
                arrive(j, source, pieces[0], factors[1])[0].start()

        for number, piece in enumerate(pieces):

            @pl.when((place[j] == number) & (sel[j] < SOURCES - 1))
            def _():
                for copy in arrive(j, sources[0], piece, factors[1 + number // 2])[1:]:
                    copy.start()

    for j in range(steps):

        @pl.when(sel[j] < SOURCES - 1)
        def _():
            for copy in arrive(j, sources[0], pieces[0], factors[1]):
                copy.wait()
            term = dot(line[j], weight[j])
            if j == 0:
                total[...] = term
            else:
                total[...] += term


def rest_kernel(farthest, total, block, other, *refs):
    pieces, refs = refs[:4], refs[4:]
    factors, refs = refs[:3], refs[3:]
    stored, adapter, fold, partial, shrunk, weight, sems = refs
    depth, width = pieces[0].shape
    columns = factors[0].shape[1]
    own_rows = pl.ds(pl.multiple_of(farthest[0] * depth, depth), depth)
    tail_rows = pl.ds(pl.multiple_of(lax.rem(farthest[0], 2) * depth, depth), depth)

    def arrive(piece, tail):
        return [
            pltpu.make_async_copy(piece, weight.at[:, pl.ds(0, width)], sems.at[0]),
            pltpu.make_async_copy(
                factors[0].at[own_rows], weight.at[:, pl.ds(width, columns)], sems.at[1]
            ),
            pltpu.make_async_copy(
                tail.at[tail_rows], weight.at[:, pl.ds(width + columns, columns)], sems.at[2]
            ),
        ]

    for number, piece in enumerate(pieces):

        @pl.when(farthest[0] == number)
        def _():
            for copy in arrive(piece, factors[1 + number // 2]):
                copy.start()

    for copy in arrive(pieces[0], factors[1]):
        copy.wait()
    full = total[...] + dot(block[...] + other[...], weight[...])
    partial[...] = full[:, :width].astype(partial.dtype)
    kept = jnp.where(stored[...] == adapter[...], full[:, width:], 0.0).astype(jnp.bfloat16)
    across = (((1,), (1,)), ((), ()))
    shrunk[...] = lax.dot_general(
        fold[...], kept, across, preferred_element_type=jnp.float32
    ).astype(shrunk.dtype)


def own_kernel(sel, place, *refs):
    sources, refs = refs[: SOURCES - 1], refs[SOURCES - 1 :]
    halves, (base, line, weight, sems) = refs[:2], refs[2:]
    depth = sources[0].shape[1]
    steps = sel.shape[0]

    def copies(j, source, half):
        rows = pl.ds(pl.multiple_of(lax.rem(place[j], 2) * depth, depth), depth)
        return [
            pltpu.make_async_copy(source, line.at[j], sems.at[j, 0]),
            pltpu.make_async_copy(half.at[rows], weight.at[j], sems.at[j, 1]),
        ]

    for j in range(steps):
        for number, source in enumerate(sources):

            @pl.when(sel[j] == number)
            def _():
                copies(j, source, halves[0])[0].start()

        for number, half in enumerate(halves):

            @pl.when((place[j] // 2 == number) & (sel[j] < SOURCES - 1))
            def _():
                copies(j, sources[0], half)[1].start()

    for j in range(steps):

        @pl.when(sel[j] < SOURCES - 1)
        def _():
            for copy in copies(j, sources[0], halves[0]):
                copy.wait()
            term = dot(line[j], weight[j])
            if j == 0:
                base[...] = term
            else:
                base[...] += term


def lora_kernel(farthest, base, everyone, stored, adapter, unfold, *refs):
    expand, (block, other), weights, refs = refs[:2], refs[2:4], refs[4:6], refs[6:]
    partials, (out, weight, sem) = refs[:-3], refs[-3:]
    depth = weight.shape[0]
    rows = pl.ds(pl.multiple_of(farthest[0] * depth, depth), depth)
    for number, half in enumerate(weights):

        @pl.when(farthest[1] == number)
        def _():
            pltpu.make_async_copy(half.at[rows], weight, sem).start()

    shrunk = jnp.sum(everyone[...].astype(jnp.float32), axis=0).astype(jnp.bfloat16)
    spread = lax.dot_general(
        shrunk, unfold[...], (((0,), (0,)), ((), ())), preferred_element_type=jnp.float32
    )
    spread = jnp.where(stored[...] == adapter[...], spread, 0.0).astype(jnp.bfloat16)
    half = spread.shape[1] // 2
    added = dot(spread[:, :half], expand[0][...]) + dot(spread[:, half:], expand[1][...])
    pltpu.make_async_copy(weights[0].at[rows], weight, sem).wait()
    added = base[...] + added + dot(block[...] + other[...], weight[...])
    for partial in partials:
        added += partial[...].astype(jnp.float32)
    out[...] = added.astype(out.dtype)


def sum_kernel(base, partial, *refs):
    refs[-1][...] = (base[...] + partial[...].astype(jnp.float32)).astype(jnp.bfloat16)


def whole(shape):
    return pl.BlockSpec(shape, lambda n, *_: (0,) * len(shape))


def on_line(kernel, scalars, sources, weights, small, outs, scratch):
    rows, depth = sources[0].shape
    planes = scalars[0].shape[0]
    width = weights[0].shape[-1]
    flops = 2 * rows * planes * depth * width
    size = 2 * planes * depth * width + 2 * rows * planes * depth + 4 * rows * width
    return pl.pallas_call(
        kernel,
        grid_spec=pltpu.PrefetchScalarGridSpec(
            num_scalar_prefetch=2,
            grid=(1,),
            in_specs=[pl.BlockSpec(memory_space=pl.ANY) for _ in sources + weights]
            + [whole(v.shape) for v in small],
            out_specs=[whole(o.shape) for o in outs],
            scratch_shapes=scratch + [pltpu.SemaphoreType.DMA((planes, 4))],
        ),
        out_shape=outs,
        compiler_params=pltpu.CompilerParams(vmem_limit_bytes=VMEM_BYTES),
        cost_estimate=pl.CostEstimate(flops=flops, bytes_accessed=size, transcendentals=0),
    )(*scalars, *sources, *weights, *small)


def after(value, *events):
    return lax.optimization_barrier((value,) + events)[0]


def line_body(
    tokens, query_weight, shrink_factors, expand_factors, row_adapter_index, adapter_storage_block
):
    tp = lax.axis_size("tp")
    planes = tp // 2
    own = lax.axis_index("tp")
    z, x = own // 2, own % 2
    r, d = lax.axis_index("rep"), lax.axis_index("dp")
    rows, depth = tokens.shape
    width = query_weight.shape[1]
    holder_columns = shrink_factors.shape[1]
    holder_adapters = holder_columns // ADAPTER_RANK
    half = holder_columns // 2
    across = [(i, i ^ 1) for i in range(tp)]
    swap = [(0, 1), (1, 0)]

    def up(h):
        return [(i, i + 2) for i in range(2 * (h - 1), tp - 2)]

    def down(h):
        return [(i + 2, i) for i in range(0, tp - 2 * h)]

    def place(plane):
        return 2 * ((plane // 2) ^ d) + ((plane % 2) ^ r)

    def plane_at(p):
        return 2 * ((p // 2) ^ d) + ((p % 2) ^ r)

    pieces, starts = [], []
    first = 0
    for count in ROW_CHUNKS:
        starts.append(first)
        pieces.append(tokens[first : first + count])
        first += count
    ups = [{0: p} for p in pieces]
    downs = [{0: p} for p in pieces]

    def hop(c, h):
        ups[c][h] = lax.ppermute(ups[c][h - 1], "tp", up(h))
        downs[c][h] = lax.ppermute(downs[c][h - 1], "tp", down(h))

    def step(values, *events):
        return lax.optimization_barrier((values, events))[0]

    def to_other_core(value):
        return lax.ppermute(value, "dp", swap)

    steps = jnp.arange(planes)
    above = z + steps < planes
    hops = jnp.where(above, steps, planes - steps)
    sel = jnp.where(
        steps == 0, 0, jnp.where(hops == planes - 1, SOURCES - 1, hops + jnp.where(above, planes - 2, 0))
    ).astype(jnp.int32)
    plane = (z + steps) % planes
    places_other = place(plane).astype(jnp.int32)
    places_own = (2 * ((plane // 2) ^ d) + plane % 2).astype(jnp.int32)
    distant = jnp.where(z == 0, planes - 1, 0)
    farthest_other = place(distant).astype(jnp.int32)[None]
    farthest_own = jnp.stack([distant % 2, (distant // 2) ^ d]).astype(jnp.int32)

    blocks = query_weight.reshape(planes, depth, width)
    hop(0, 1)
    hop(1, 1)
    near = lax.ppermute(pick(blocks, 2 * r + (1 - x)), "tp", across)

    factors = shrink_factors.reshape(planes, 2, depth, holder_columns)
    leaving = jnp.concatenate([pick(pick(factors, plane_at(p)), 1 - x) for p in range(planes // 2)])
    expand_half = lax.dynamic_slice_in_dim(expand_factors, d * half, half, 0)
    expand_half = expand_half.reshape(half, tp, width).transpose(1, 0, 2)
    (ups[0][1], downs[0][1], ups[1][1], downs[1][1], near, leaving, weights, factors, expand_half) = step(
        (ups[0][1], downs[0][1], ups[1][1], downs[1][1], near, leaving, query_weight, factors, expand_half)
    )
    hop(0, 2)
    far = lax.ppermute(near, "rep", swap)
    shrink_near = lax.ppermute(leaving, "tp", across)
    near_crossed = to_other_core(near)
    pairs = weights.reshape(planes // 2, 2, depth, width)
    own_half = lax.dynamic_index_in_dim(pairs, x, 1, keepdims=False).reshape(-1, width)
    shrink_own = jnp.concatenate([pick(pick(factors, plane_at(p)), x) for p in range(planes)])
    expand_half = lax.all_to_all(expand_half, "tp", split_axis=0, concat_axis=0, tiled=True)
    expand_half = expand_half.reshape(tp * half, width)

    (ups[0][2], downs[0][2], ups[1][1], downs[1][1], shrink_near, far, near_crossed, expand_half, own_half, shrink_own, sel, places_other, places_own) = step(
        (ups[0][2], downs[0][2], ups[1][1], downs[1][1], shrink_near, far, near_crossed, expand_half, own_half, shrink_own, sel, places_other, places_own)
    )
    hop(0, 3)
    shrink = [shrink_own, shrink_near, to_other_core(shrink_near)]
    weight_other = [near, far, near_crossed, to_other_core(far)]
    weight_own = [own_half, to_other_core(own_half)]

    known = jnp.arange(adapter_storage_block.shape[0])
    stored = jnp.sum(
        jnp.where(row_adapter_index == known[None, :], adapter_storage_block[None, :], 0),
        axis=1,
        keepdims=True,
    )
    column = jnp.arange(2 * holder_columns)
    column_adapter = (own ^ (column // holder_columns)) * holder_adapters + (
        column % holder_columns
    ) // ADAPTER_RANK
    column_adapter = column_adapter[None, :].astype(jnp.int32)
    fold = (jnp.arange(ADAPTER_RANK)[:, None] == column[None, :] % ADAPTER_RANK).astype(jnp.bfloat16)
    entry = jnp.arange(tp * holder_columns)
    within = entry % (tp * half)
    entry_adapter = (within // half) * holder_adapters + (
        ((entry // (tp * half)) ^ d) * half + within % half
    ) // ADAPTER_RANK
    entry_adapter = entry_adapter[None, :].astype(jnp.int32)
    unfold = (jnp.arange(ADAPTER_RANK)[:, None] == entry[None, :] % ADAPTER_RANK).astype(jnp.bfloat16)

    def sources(c):
        between = range(1, planes - 1)
        return [pieces[c]] + [ups[c][h] for h in between] + [downs[c][h] for h in between] + [
            None
        ]

    def longest(c):
        return ups[c][planes - 1], downs[c][planes - 1]

    total_columns = width + 2 * holder_columns

    def early_part(c, *events):
        count = ROW_CHUNKS[c]
        return on_line(
            early_kernel,
            [after(sel, *events) if events else sel, places_other],
            sources(c)[:-1],
            weight_other + shrink,
            [],
            [jax.ShapeDtypeStruct((count, total_columns), jnp.float32)],
            [
                pltpu.VMEM((planes, count, depth), jnp.bfloat16),
                pltpu.VMEM((planes, depth, total_columns), jnp.bfloat16),
            ],
        )[0]

    def rest_part(c, total):
        count = ROW_CHUNKS[c]
        small = [stored[starts[c] : starts[c] + count], column_adapter, fold]
        outs = [
            jax.ShapeDtypeStruct((count, width), jnp.bfloat16),
            jax.ShapeDtypeStruct((ADAPTER_RANK, count), jnp.bfloat16),
        ]
        return pl.pallas_call(
            rest_kernel,
            grid_spec=pltpu.PrefetchScalarGridSpec(
                num_scalar_prefetch=1,
                grid=(1,),
                in_specs=[whole(total.shape), whole((count, depth)), whole((count, depth))]
                + [pl.BlockSpec(memory_space=pl.ANY) for _ in range(7)]
                + [whole(v.shape) for v in small],
                out_specs=[whole(o.shape) for o in outs],
                scratch_shapes=[
                    pltpu.VMEM((depth, total_columns), jnp.bfloat16),
                    pltpu.SemaphoreType.DMA((3,)),
                ],
            ),
            out_shape=outs,
            compiler_params=pltpu.CompilerParams(vmem_limit_bytes=VMEM_BYTES),
            cost_estimate=pl.CostEstimate(
                flops=2 * count * depth * total_columns, bytes_accessed=4 * depth * width, transcendentals=0
            ),
        )(farthest_other, total, *longest(c), *weight_other, *shrink, *small)

    def own_part(c, *events):
        count = ROW_CHUNKS[c]
        return on_line(
            own_kernel,
            [after(sel, *events) if events else sel, places_own],
            sources(c)[:-1],
            weight_own,
            [],
            [jax.ShapeDtypeStruct((count, width), jnp.float32)],
            [
                pltpu.VMEM((planes, count, depth), jnp.bfloat16),
                pltpu.VMEM((planes, depth, width), jnp.bfloat16),
            ],
        )[0]

    def spread_out(shrunk):
        everyone = jnp.broadcast_to(shrunk[None], (tp,) + shrunk.shape)
        return lax.all_to_all(everyone, "tp", split_axis=0, concat_axis=0, tiled=True)

    def lora_part(c, base, everyone, expand, partial=None):
        count = ROW_CHUNKS[c]
        rows_of = whole((count, width))
        partials = [] if partial is None else [partial]
        out = (count, width, jnp.float32) if partial is None else (rows, width, jnp.bfloat16)
        return pl.pallas_call(
            lora_kernel,
            grid_spec=pltpu.PrefetchScalarGridSpec(
                num_scalar_prefetch=1,
                grid=(1,),
                in_specs=[
                    rows_of,
                    whole(everyone.shape),
                    whole((count, 1)),
                    whole(entry_adapter.shape),
                    whole(unfold.shape),
                    whole(expand[0].shape),
                    whole(expand[1].shape),
                    whole((count, depth)),
                    whole((count, depth)),
                ]
                + [pl.BlockSpec(memory_space=pl.ANY)] * 2
                + [rows_of for _ in partials],
                out_specs=rows_of,
                scratch_shapes=[pltpu.VMEM((depth, width), jnp.bfloat16), pltpu.SemaphoreType.DMA],
            ),
            out_shape=jax.ShapeDtypeStruct(out[:2], out[2]),
            compiler_params=pltpu.CompilerParams(vmem_limit_bytes=VMEM_BYTES),
            cost_estimate=pl.CostEstimate(
                flops=4 * count * width * depth, bytes_accessed=4 * depth * width, transcendentals=0
            ),
        )(
            farthest_own,
            base,
            everyone,
            stored[starts[c] : starts[c] + count],
            entry_adapter,
            unfold,
            *expand,
            *longest(c),
            *weight_own,
            *partials,
        )

    def sum_part(c, base, partial, earlier):
        count, step = ROW_CHUNKS[c], ROW_STEP
        here = starts[c] // step
        rows_of = pl.BlockSpec((step, width), lambda i: (i, 0))
        operands = [base, partial, earlier]
        specs = [rows_of, rows_of, pl.BlockSpec(memory_space=pl.ANY)]
        aliases = {2: 0}
        return pl.pallas_call(
            sum_kernel,
            grid=(count // step,),
            in_specs=specs,
            out_specs=pl.BlockSpec((step, width), lambda i: (i + here, 0)),
            out_shape=jax.ShapeDtypeStruct((rows, width), jnp.bfloat16),
            input_output_aliases=aliases,
            compiler_params=pltpu.CompilerParams(vmem_limit_bytes=VMEM_BYTES),
            cost_estimate=pl.CostEstimate(
                flops=2 * count * width, bytes_accessed=8 * count * width, transcendentals=0
            ),
        )(*operands)

    early_a = early_part(0)
    base_a = own_part(0, early_a)
    (ups[0][3], ups[1][1], downs[1][1], expand_half) = step(
        (ups[0][3], ups[1][1], downs[1][1], expand_half), base_a
    )
    hop(1, 2)
    expand = [expand_half, to_other_core(expand_half)]
    partial_a, shrunk_a = rest_part(0, early_a)
    got_a = lax.ppermute(partial_a, "tp", across)
    ups[1][2], downs[1][2] = step((ups[1][2], downs[1][2]), partial_a)
    hop(1, 3)
    everyone_a = spread_out(shrunk_a)
    early_c = early_part(1)
    base_c = own_part(1, early_c)
    ups[1][3], downs[1][3] = step((ups[1][3], downs[1][3]), base_c, got_a, everyone_a)
    partial_c, shrunk_c = rest_part(1, early_c)
    got_c = lax.ppermute(partial_c, "tp", across)
    everyone_c = spread_out(shrunk_c)
    out = lora_part(0, base_a, everyone_a, expand, got_a)
    whole_c = lora_part(1, base_c, everyone_c, expand)
    return sum_part(1, whole_c, got_c, out)


def solution(mesh):
    placed = (
        P(("rep", "dp"), "tp"),
        P("dp", "tp"),
        P(None, ("rep", "tp")),
        P(("rep", "tp"), None),
        P(("rep", "dp"), None),
        P("rep"),
    )
    lined = dict(mesh.shape) == {"rep": 2, "tp": 8, "dp": 2}
    return jax.shard_map(
        line_body if lined else general_body,
        mesh=mesh,
        in_specs=placed,
        out_specs=P(("rep", "dp"), "tp"),
        check_vma=False,
    )
```

```python
import functools

import jax
import jax.numpy as jnp
from jax import lax
from jax.experimental import pallas as pl
from jax.experimental.pallas import tpu as pltpu
from jax.sharding import PartitionSpec as P

ADAPTER_RANK = 16
ROW_CHUNKS = (640, 384)
SOURCES = 6
VMEM_BYTES = 56 * 1024 * 1024


def general_body(
    tokens, query_weight, shrink_factors, expand_factors, row_adapter_index, adapter_storage_block
):
    holder_count = lax.axis_size("tp")
    own_index = lax.axis_index("tp")
    rows_per_holder = shrink_factors.shape[1] // ADAPTER_RANK
    row_count = tokens.shape[0]
    capacity = 2 * row_count // holder_count
    full_rows = lax.all_gather(tokens, "tp", axis=1, tiled=True)
    weight = lax.all_gather(query_weight, "dp", axis=0, tiled=True)
    base_output = jnp.dot(full_rows, weight, preferred_element_type=jnp.float32)
    storage_weights = jnp.take(adapter_storage_block, row_adapter_index[:, 0])
    owner_of = storage_weights // rows_per_holder
    local_of = storage_weights % rows_per_holder
    onehot = (owner_of[:, None] == jnp.arange(holder_count)[None, :]).astype(jnp.int32)
    rank_in_owner = jnp.sum(jnp.cumsum(onehot, axis=0) * onehot, axis=1) - 1
    select = (owner_of[None, :] == own_index) & (
        rank_in_owner[None, :] == jnp.arange(capacity)[:, None]
    )
    selected_rows = jnp.dot(
        select.astype(jnp.bfloat16), full_rows, preferred_element_type=jnp.float32
    ).astype(jnp.bfloat16)
    picked_local = jnp.sum(select.astype(jnp.int32) * local_of[None, :], axis=1)
    reduced_rows = jnp.dot(selected_rows, shrink_factors, preferred_element_type=jnp.float32)
    column_block = jnp.arange(rows_per_holder * ADAPTER_RANK) // ADAPTER_RANK
    keep_mask = column_block[None, :] == picked_local[:, None]
    masked = jnp.where(keep_mask, reduced_rows, 0.0)
    compact = jnp.sum(masked.reshape(capacity, rows_per_holder, ADAPTER_RANK), axis=1)
    spread = jnp.dot(select.T.astype(jnp.float32), compact, precision=lax.Precision.HIGHEST)
    shrink_all = lax.psum(spread, "tp").astype(jnp.bfloat16)
    columns = lax.all_to_all(
        expand_factors.reshape(rows_per_holder * ADAPTER_RANK, holder_count, -1),
        "tp",
        split_axis=1,
        concat_axis=0,
        tiled=True,
    )
    columns = columns.reshape(holder_count * rows_per_holder, ADAPTER_RANK, -1)
    factor_rows = jnp.take(columns, storage_weights, axis=0)
    adapter_output = jnp.einsum(
        "tr,trc->tc", shrink_all, factor_rows, preferred_element_type=jnp.float32
    ).astype(jnp.bfloat16)
    adapter_output = lax.optimization_barrier(adapter_output)
    return (base_output + adapter_output.astype(jnp.float32)).astype(jnp.bfloat16)


def dot(a, b):
    return jnp.dot(a, b, preferred_element_type=jnp.float32)


def pick(a, j):
    return lax.dynamic_index_in_dim(a, j, 0, keepdims=False)


def early_kernel(sel, place, *refs):
    sources, refs = refs[: SOURCES - 1], refs[SOURCES - 1 :]
    pieces, refs = refs[:4], refs[4:]
    factors, (total, line, weight, sems) = refs[:3], refs[3:]
    depth, width = pieces[0].shape
    columns, half = factors[0].shape[1], factors[1].shape[0]
    steps = sel.shape[0]

    def arrive(j, source, piece, tail):
        own_rows = pl.ds(pl.multiple_of(place[j] * depth, depth), depth)
        tail_rows = pl.ds(pl.multiple_of(lax.rem(place[j], 2) * depth, depth), depth)
        return [
            pltpu.make_async_copy(source, line.at[j], sems.at[j, 0]),
            pltpu.make_async_copy(piece, weight.at[j, :, pl.ds(0, width)], sems.at[j, 1]),
            pltpu.make_async_copy(
                factors[0].at[own_rows], weight.at[j, :, pl.ds(width, columns)], sems.at[j, 2]
            ),
            pltpu.make_async_copy(
                tail.at[tail_rows], weight.at[j, :, pl.ds(width + columns, columns)], sems.at[j, 3]
            ),
        ]

    for j in range(steps):
        for number, source in enumerate(sources):

            @pl.when(sel[j] == number)
            def _():
                arrive(j, source, pieces[0], factors[1])[0].start()

        for number, piece in enumerate(pieces):

            @pl.when((place[j] == number) & (sel[j] < SOURCES - 1))
            def _():
                for copy in arrive(j, sources[0], piece, factors[1 + number // 2])[1:]:
                    copy.start()

    for j in range(steps):

        @pl.when(sel[j] < SOURCES - 1)
        def _():
            for copy in arrive(j, sources[0], pieces[0], factors[1]):
                copy.wait()
            term = dot(line[j], weight[j])
            if j == 0:
                total[...] = term
            else:
                total[...] += term


def rest_kernel(farthest, *refs):
    total, blocks, pieces, factors, refs = refs[0], refs[1:3], refs[3:7], refs[7:10], refs[10:]
    stored, adapter, fold, partial, shrunk, sums, line, weight, sems = refs
    depth, width = pieces[0].shape
    columns = factors[0].shape[1]
    own_rows = pl.ds(pl.multiple_of(farthest[0] * depth, depth), depth)
    tail_rows = pl.ds(pl.multiple_of(lax.rem(farthest[0], 2) * depth, depth), depth)
    lines = [pltpu.make_async_copy(v, line.at[q], sems.at[q]) for q, v in enumerate(blocks)]

    def arrive(piece, tail):
        return [
            pltpu.make_async_copy(piece, weight.at[:, pl.ds(0, width)], sems.at[2]),
            pltpu.make_async_copy(
                factors[0].at[own_rows], weight.at[:, pl.ds(width, columns)], sems.at[3]
            ),
            pltpu.make_async_copy(
                tail.at[tail_rows], weight.at[:, pl.ds(width + columns, columns)], sems.at[4]
            ),
        ]

    for copy in lines:
        copy.start()
    for number, piece in enumerate(pieces):

        @pl.when(farthest[0] == number)
        def _():
            for copy in arrive(piece, factors[1 + number // 2]):
                copy.start()

    before = pltpu.make_async_copy(total, sums, sems.at[5])
    before.start()
    for copy in lines + arrive(pieces[0], factors[1]):
        copy.wait()
    term = dot(line[0] + line[1], weight[...])
    before.wait()
    full = sums[...] + term
    partial[...] = full[:, :width].astype(partial.dtype)
    kept = jnp.where(stored[...] == adapter[...], full[:, width:], 0.0).astype(jnp.bfloat16)
    across = (((1,), (1,)), ((), ()))
    small = lax.dot_general(fold[...], kept, across, preferred_element_type=jnp.float32)
    for q in range(shrunk.shape[0]):
        shrunk[q] = small.astype(shrunk.dtype)


def own_kernel(sel, place, *refs):
    sources, refs = refs[: SOURCES - 1], refs[SOURCES - 1 :]
    halves, (base, line, weight, sems) = refs[:2], refs[2:]
    depth = sources[0].shape[1]
    steps = sel.shape[0]

    def copies(j, source, half):
        rows = pl.ds(pl.multiple_of(lax.rem(place[j], 2) * depth, depth), depth)
        return [
            pltpu.make_async_copy(source, line.at[j], sems.at[j, 0]),
            pltpu.make_async_copy(half.at[rows], weight.at[j], sems.at[j, 1]),
        ]

    for j in range(steps):
        for number, source in enumerate(sources):

            @pl.when(sel[j] == number)
            def _():
                copies(j, source, halves[0])[0].start()

        for number, half in enumerate(halves):

            @pl.when((place[j] // 2 == number) & (sel[j] < SOURCES - 1))
            def _():
                copies(j, sources[0], half)[1].start()

    for j in range(steps):

        @pl.when(sel[j] < SOURCES - 1)
        def _():
            for copy in copies(j, sources[0], halves[0]):
                copy.wait()
            term = dot(line[j], weight[j])
            if j == 0:
                base[...] = term
            else:
                base[...] += term


def last_kernel(start, farthest, everyone, stored, adapter, unfold, *refs):
    base, partial, expand, blocks, weights, refs = (
        refs[0], refs[1], refs[2:4], refs[4:6], refs[6:8], refs[8:],
    )
    out, sums, added, factor, line, weight, result, sems = refs[-8:]
    depth = weight.shape[0]
    rows = pl.ds(pl.multiple_of(farthest[0] * depth, depth), depth)
    factors = [pltpu.make_async_copy(v, factor.at[q], sems.at[q]) for q, v in enumerate(expand)]
    lines = [pltpu.make_async_copy(v, line.at[q], sems.at[2 + q]) for q, v in enumerate(blocks)]
    others = [
        pltpu.make_async_copy(base, sums, sems.at[5]),
        pltpu.make_async_copy(partial, added, sems.at[6]),
    ]
    for copy in factors + lines:
        copy.start()
    for number, half in enumerate(weights):

        @pl.when(farthest[1] == number)
        def _():
            pltpu.make_async_copy(half.at[rows], weight, sems.at[4]).start()

    for copy in others:
        copy.start()
    shrunk = jnp.sum(everyone[...].astype(jnp.float32), axis=0).astype(jnp.bfloat16)
    spread = lax.dot_general(
        shrunk, unfold[...], (((0,), (0,)), ((), ())), preferred_element_type=jnp.float32
    )
    spread = jnp.where(stored[...] == adapter[...], spread, 0.0).astype(jnp.bfloat16)
    half = spread.shape[1] // 2
    for copy in factors:
        copy.wait()
    total = dot(spread[:, :half], factor[0]) + dot(spread[:, half:], factor[1])
    for copy in lines:
        copy.wait()
    pltpu.make_async_copy(weights[0].at[rows], weight, sems.at[4]).wait()
    total += dot(line[0] + line[1], weight[...])
    for copy in others:
        copy.wait()
    result[...] = (total + sums[...] + added[...].astype(jnp.float32)).astype(result.dtype)
    copy = pltpu.make_async_copy(result, out.at[pl.ds(start, result.shape[0])], sems.at[7])
    copy.start()
    copy.wait()


def whole(shape):
    return pl.BlockSpec(shape, lambda n, *_: (0,) * len(shape))


def on_line(kernel, scalars, sources, weights, small, outs, scratch):
    rows, depth = sources[0].shape
    planes = scalars[0].shape[0]
    width = weights[0].shape[-1]
    flops = 2 * rows * planes * depth * width
    size = 2 * planes * depth * width + 2 * rows * planes * depth + 4 * rows * width
    return pl.pallas_call(
        kernel,
        grid_spec=pltpu.PrefetchScalarGridSpec(
            num_scalar_prefetch=2,
            grid=(1,),
            in_specs=[pl.BlockSpec(memory_space=pl.ANY) for _ in sources + weights]
            + [whole(v.shape) for v in small],
            out_specs=[whole(o.shape) for o in outs],
            scratch_shapes=scratch + [pltpu.SemaphoreType.DMA((planes, 4))],
        ),
        out_shape=outs,
        compiler_params=pltpu.CompilerParams(vmem_limit_bytes=VMEM_BYTES),
        cost_estimate=pl.CostEstimate(flops=flops, bytes_accessed=size, transcendentals=0),
    )(*scalars, *sources, *weights, *small)


def after(value, *events):
    return lax.optimization_barrier((value,) + events)[0]


def line_body(
    tokens, query_weight, shrink_factors, expand_factors, row_adapter_index, adapter_storage_block
):
    tp = lax.axis_size("tp")
    planes = tp // 2
    own = lax.axis_index("tp")
    z, x = own // 2, own % 2
    r, d = lax.axis_index("rep"), lax.axis_index("dp")
    rows, depth = tokens.shape
    width = query_weight.shape[1]
    holder_columns = shrink_factors.shape[1]
    holder_adapters = holder_columns // ADAPTER_RANK
    half = holder_columns // 2
    across = [(i, i ^ 1) for i in range(tp)]
    swap = [(0, 1), (1, 0)]

    def up(h):
        return [(i, i + 2) for i in range(2 * (h - 1), tp - 2)]

    def down(h):
        return [(i + 2, i) for i in range(0, tp - 2 * h)]

    def place(plane):
        return 2 * ((plane // 2) ^ d) + ((plane % 2) ^ r)

    def plane_at(p):
        return 2 * ((p // 2) ^ d) + ((p % 2) ^ r)

    pieces, starts = [], []
    first = 0
    for count in ROW_CHUNKS:
        starts.append(first)
        pieces.append(tokens[first : first + count])
        first += count
    ups = [{0: p} for p in pieces]
    downs = [{0: p} for p in pieces]

    def hop(c, h):
        ups[c][h] = lax.ppermute(ups[c][h - 1], "tp", up(h))
        downs[c][h] = lax.ppermute(downs[c][h - 1], "tp", down(h))

    def step(values, *events):
        return lax.optimization_barrier((values, events))[0]

    def to_other_core(value):
        return lax.ppermute(value, "dp", swap)

    steps = jnp.arange(planes)
    above = z + steps < planes
    hops = jnp.where(above, steps, planes - steps)
    sel = jnp.where(
        steps == 0, 0, jnp.where(hops == planes - 1, SOURCES - 1, hops + jnp.where(above, planes - 2, 0))
    ).astype(jnp.int32)
    plane = (z + steps) % planes
    places_other = place(plane).astype(jnp.int32)
    places_own = (2 * ((plane // 2) ^ d) + plane % 2).astype(jnp.int32)
    distant = jnp.where(z == 0, planes - 1, 0)
    farthest_other = place(distant).astype(jnp.int32)[None]
    farthest_own = jnp.stack([distant % 2, (distant // 2) ^ d]).astype(jnp.int32)

    blocks = query_weight.reshape(planes, depth, width)
    hop(0, 1)
    hop(1, 1)
    near = lax.ppermute(pick(blocks, 2 * r + (1 - x)), "tp", across)

    factors = shrink_factors.reshape(planes, 2, depth, holder_columns)
    leaving = jnp.concatenate([pick(pick(factors, plane_at(p)), 1 - x) for p in range(planes // 2)])
    expand_half = lax.dynamic_slice_in_dim(expand_factors, d * half, half, 0)
    expand_half = expand_half.reshape(half, tp, width).transpose(1, 0, 2)
    (ups[0][1], downs[0][1], ups[1][1], downs[1][1], near, leaving, weights, factors, expand_half) = step(
        (ups[0][1], downs[0][1], ups[1][1], downs[1][1], near, leaving, query_weight, factors, expand_half)
    )
    hop(0, 2)
    far = lax.ppermute(near, "rep", swap)
    shrink_near = lax.ppermute(leaving, "tp", across)
    near_crossed = to_other_core(near)
    pairs = weights.reshape(planes // 2, 2, depth, width)
    own_half = lax.dynamic_index_in_dim(pairs, x, 1, keepdims=False).reshape(-1, width)
    shrink_own = jnp.concatenate([pick(pick(factors, plane_at(p)), x) for p in range(planes)])
    expand_half = lax.all_to_all(expand_half, "tp", split_axis=0, concat_axis=0, tiled=True)
    expand_half = expand_half.reshape(tp * half, width)

    (ups[0][2], downs[0][2], ups[1][1], downs[1][1], shrink_near, far, near_crossed, expand_half, own_half, shrink_own, sel, places_other, places_own) = step(
        (ups[0][2], downs[0][2], ups[1][1], downs[1][1], shrink_near, far, near_crossed, expand_half, own_half, shrink_own, sel, places_other, places_own)
    )
    hop(0, 3)
    shrink = [shrink_own, shrink_near, to_other_core(shrink_near)]
    weight_other = [near, far, near_crossed, to_other_core(far)]
    weight_own = [own_half, to_other_core(own_half)]

    known = jnp.arange(adapter_storage_block.shape[0])
    stored = jnp.sum(
        jnp.where(row_adapter_index == known[None, :], adapter_storage_block[None, :], 0),
        axis=1,
        keepdims=True,
    )
    column = jnp.arange(2 * holder_columns)
    column_adapter = (own ^ (column // holder_columns)) * holder_adapters + (
        column % holder_columns
    ) // ADAPTER_RANK
    column_adapter = column_adapter[None, :].astype(jnp.int32)
    fold = (jnp.arange(ADAPTER_RANK)[:, None] == column[None, :] % ADAPTER_RANK).astype(jnp.bfloat16)
    entry = jnp.arange(tp * holder_columns)
    within = entry % (tp * half)
    entry_adapter = (within // half) * holder_adapters + (
        ((entry // (tp * half)) ^ d) * half + within % half
    ) // ADAPTER_RANK
    entry_adapter = entry_adapter[None, :].astype(jnp.int32)
    unfold = (jnp.arange(ADAPTER_RANK)[:, None] == entry[None, :] % ADAPTER_RANK).astype(jnp.bfloat16)

    def sources(c):
        between = range(1, planes - 1)
        return [pieces[c]] + [ups[c][h] for h in between] + [downs[c][h] for h in between] + [
            None
        ]

    def longest(c):
        return ups[c][planes - 1], downs[c][planes - 1]

    total_columns = width + 2 * holder_columns

    def early_part(c, *events):
        count = ROW_CHUNKS[c]
        return on_line(
            early_kernel,
            [after(sel, *events) if events else sel, places_other],
            sources(c)[:-1],
            weight_other + shrink,
            [],
            [jax.ShapeDtypeStruct((count, total_columns), jnp.float32)],
            [
                pltpu.VMEM((planes, count, depth), jnp.bfloat16),
                pltpu.VMEM((planes, depth, total_columns), jnp.bfloat16),
            ],
        )[0]

    def rest_part(c, total):
        count = ROW_CHUNKS[c]
        small = [stored[starts[c] : starts[c] + count], column_adapter, fold]
        outs = [
            jax.ShapeDtypeStruct((count, width), jnp.bfloat16),
            jax.ShapeDtypeStruct((tp, ADAPTER_RANK, count), jnp.bfloat16),
        ]
        return pl.pallas_call(
            rest_kernel,
            grid_spec=pltpu.PrefetchScalarGridSpec(
                num_scalar_prefetch=1,
                grid=(1,),
                in_specs=[pl.BlockSpec(memory_space=pl.ANY) for _ in range(10)]
                + [whole(v.shape) for v in small],
                out_specs=[whole(o.shape) for o in outs],
                scratch_shapes=[
                    pltpu.VMEM((count, total_columns), jnp.float32),
                    pltpu.VMEM((2, count, depth), jnp.bfloat16),
                    pltpu.VMEM((depth, total_columns), jnp.bfloat16),
                    pltpu.SemaphoreType.DMA((6,)),
                ],
            ),
            out_shape=outs,
            compiler_params=pltpu.CompilerParams(vmem_limit_bytes=VMEM_BYTES),
            cost_estimate=pl.CostEstimate(
                flops=2 * count * depth * total_columns, bytes_accessed=4 * depth * width, transcendentals=0
            ),
        )(farthest_other, total, *longest(c), *weight_other, *shrink, *small)

    def own_part(c, *events):
        count = ROW_CHUNKS[c]
        return on_line(
            own_kernel,
            [after(sel, *events) if events else sel, places_own],
            sources(c)[:-1],
            weight_own,
            [],
            [jax.ShapeDtypeStruct((count, width), jnp.float32)],
            [
                pltpu.VMEM((planes, count, depth), jnp.bfloat16),
                pltpu.VMEM((planes, depth, width), jnp.bfloat16),
            ],
        )[0]

    def spread_out(shrunk):
        return lax.all_to_all(shrunk, "tp", split_axis=0, concat_axis=0, tiled=True)

    def last_part(c, base, partial, everyone, expand, earlier):
        count = ROW_CHUNKS[c]
        hbm = [base, partial, *expand, *longest(c), *weight_own]
        aliases = {}
        if earlier is not None:
            aliases = {5 + len(hbm): 0}
            hbm.append(earlier)
        return pl.pallas_call(
            functools.partial(last_kernel, starts[c]),
            grid_spec=pltpu.PrefetchScalarGridSpec(
                num_scalar_prefetch=1,
                grid=(1,),
                in_specs=[
                    whole(everyone.shape),
                    whole((count, 1)),
                    whole(entry_adapter.shape),
                    whole(unfold.shape),
                ]
                + [pl.BlockSpec(memory_space=pl.ANY) for _ in hbm],
                out_specs=pl.BlockSpec(memory_space=pl.ANY),
                scratch_shapes=[
                    pltpu.VMEM((count, width), jnp.float32),
                    pltpu.VMEM((count, width), jnp.bfloat16),
                    pltpu.VMEM((2,) + expand[0].shape, jnp.bfloat16),
                    pltpu.VMEM((2, count, depth), jnp.bfloat16),
                    pltpu.VMEM((depth, width), jnp.bfloat16),
                    pltpu.VMEM((count, width), jnp.bfloat16),
                    pltpu.SemaphoreType.DMA((8,)),
                ],
            ),
            out_shape=jax.ShapeDtypeStruct((rows, width), jnp.bfloat16),
            input_output_aliases=aliases,
            compiler_params=pltpu.CompilerParams(vmem_limit_bytes=VMEM_BYTES),
            cost_estimate=pl.CostEstimate(
                flops=4 * count * width * depth, bytes_accessed=4 * depth * width, transcendentals=0
            ),
        )(
            farthest_own,
            everyone,
            stored[starts[c] : starts[c] + count],
            entry_adapter,
            unfold,
            *hbm,
        )

    early_a = early_part(0)
    base_a = own_part(0, early_a)
    (ups[0][3], ups[1][1], downs[1][1], expand_half) = step(
        (ups[0][3], ups[1][1], downs[1][1], expand_half), base_a
    )
    hop(1, 2)
    expand = [expand_half, to_other_core(expand_half)]
    partial_a, shrunk_a = rest_part(0, early_a)
    got_a = lax.ppermute(partial_a, "tp", across)
    ups[1][2], downs[1][2] = step((ups[1][2], downs[1][2]), partial_a)
    hop(1, 3)
    everyone_a = spread_out(shrunk_a)
    early_c = early_part(1)
    base_c = own_part(1, early_c)
    ups[1][3], downs[1][3] = step((ups[1][3], downs[1][3]), base_c, got_a, everyone_a)
    partial_c, shrunk_c = rest_part(1, early_c)
    got_c = lax.ppermute(partial_c, "tp", across)
    everyone_c = spread_out(shrunk_c)
    out = last_part(0, base_a, got_a, everyone_a, expand, None)
    return last_part(1, base_c, got_c, everyone_c, expand, out)


def solution(mesh):
    placed = (
        P(("rep", "dp"), "tp"),
        P("dp", "tp"),
        P(None, ("rep", "tp")),
        P(("rep", "tp"), None),
        P(("rep", "dp"), None),
        P("rep"),
    )
    lined = dict(mesh.shape) == {"rep": 2, "tp": 8, "dp": 2}
    return jax.shard_map(
        line_body if lined else general_body,
        mesh=mesh,
        in_specs=placed,
        out_specs=P(("rep", "dp"), "tp"),
        check_vma=False,
    )
```

```python
import functools

import jax
import jax.numpy as jnp
from jax import lax
from jax.experimental import pallas as pl
from jax.experimental.pallas import tpu as pltpu
from jax.sharding import PartitionSpec as P

ADAPTER_RANK = 16
ROW_CHUNKS = (640, 384)
SOURCES = 6
VMEM_BYTES = 56 * 1024 * 1024


def general_body(
    tokens, query_weight, shrink_factors, expand_factors, row_adapter_index, adapter_storage_block
):
    holder_count = lax.axis_size("tp")
    own_index = lax.axis_index("tp")
    rows_per_holder = shrink_factors.shape[1] // ADAPTER_RANK
    row_count = tokens.shape[0]
    capacity = 2 * row_count // holder_count
    full_rows = lax.all_gather(tokens, "tp", axis=1, tiled=True)
    weight = lax.all_gather(query_weight, "dp", axis=0, tiled=True)
    base_output = jnp.dot(full_rows, weight, preferred_element_type=jnp.float32)
    storage_weights = jnp.take(adapter_storage_block, row_adapter_index[:, 0])
    owner_of = storage_weights // rows_per_holder
    local_of = storage_weights % rows_per_holder
    onehot = (owner_of[:, None] == jnp.arange(holder_count)[None, :]).astype(jnp.int32)
    rank_in_owner = jnp.sum(jnp.cumsum(onehot, axis=0) * onehot, axis=1) - 1
    select = (owner_of[None, :] == own_index) & (
        rank_in_owner[None, :] == jnp.arange(capacity)[:, None]
    )
    selected_rows = jnp.dot(
        select.astype(jnp.bfloat16), full_rows, preferred_element_type=jnp.float32
    ).astype(jnp.bfloat16)
    picked_local = jnp.sum(select.astype(jnp.int32) * local_of[None, :], axis=1)
    reduced_rows = jnp.dot(selected_rows, shrink_factors, preferred_element_type=jnp.float32)
    column_block = jnp.arange(rows_per_holder * ADAPTER_RANK) // ADAPTER_RANK
    keep_mask = column_block[None, :] == picked_local[:, None]
    masked = jnp.where(keep_mask, reduced_rows, 0.0)
    compact = jnp.sum(masked.reshape(capacity, rows_per_holder, ADAPTER_RANK), axis=1)
    spread = jnp.dot(select.T.astype(jnp.float32), compact, precision=lax.Precision.HIGHEST)
    shrink_all = lax.psum(spread, "tp").astype(jnp.bfloat16)
    columns = lax.all_to_all(
        expand_factors.reshape(rows_per_holder * ADAPTER_RANK, holder_count, -1),
        "tp",
        split_axis=1,
        concat_axis=0,
        tiled=True,
    )
    columns = columns.reshape(holder_count * rows_per_holder, ADAPTER_RANK, -1)
    factor_rows = jnp.take(columns, storage_weights, axis=0)
    adapter_output = jnp.einsum(
        "tr,trc->tc", shrink_all, factor_rows, preferred_element_type=jnp.float32
    ).astype(jnp.bfloat16)
    adapter_output = lax.optimization_barrier(adapter_output)
    return (base_output + adapter_output.astype(jnp.float32)).astype(jnp.bfloat16)


def dot(a, b):
    return jnp.dot(a, b, preferred_element_type=jnp.float32)


def pick(a, j):
    return lax.dynamic_index_in_dim(a, j, 0, keepdims=False)


def early_kernel(sel, place, *refs):
    sources, refs = refs[: SOURCES - 1], refs[SOURCES - 1 :]
    pieces, refs = refs[:4], refs[4:]
    factors, (total, line, weight, sems) = refs[:3], refs[3:]
    depth, width = pieces[0].shape
    columns, half = factors[0].shape[1], factors[1].shape[0]
    steps = sel.shape[0]

    def arrive(j, source, piece, tail):
        own_rows = pl.ds(pl.multiple_of(place[j] * depth, depth), depth)
        tail_rows = pl.ds(pl.multiple_of(lax.rem(place[j], 2) * depth, depth), depth)
        return [
            pltpu.make_async_copy(source, line.at[j], sems.at[j, 0]),
            pltpu.make_async_copy(piece, weight.at[j, :, pl.ds(0, width)], sems.at[j, 1]),
            pltpu.make_async_copy(
                factors[0].at[own_rows], weight.at[j, :, pl.ds(width, columns)], sems.at[j, 2]
            ),
            pltpu.make_async_copy(
                tail.at[tail_rows], weight.at[j, :, pl.ds(width + columns, columns)], sems.at[j, 3]
            ),
        ]

    for j in range(steps):
        for number, source in enumerate(sources):

            @pl.when(sel[j] == number)
            def _():
                arrive(j, source, pieces[0], factors[1])[0].start()

        for number, piece in enumerate(pieces):

            @pl.when((place[j] == number) & (sel[j] < SOURCES - 1))
            def _():
                for copy in arrive(j, sources[0], piece, factors[1 + number // 2])[1:]:
                    copy.start()

    for j in range(steps):

        @pl.when(sel[j] < SOURCES - 1)
        def _():
            for copy in arrive(j, sources[0], pieces[0], factors[1]):
                copy.wait()
            term = dot(line[j], weight[j])
            if j == 0:
                total[...] = term
            else:
                total[...] += term


def rest_kernel(farthest, *refs):
    total, blocks, pieces, factors, refs = refs[0], refs[1:3], refs[3:7], refs[7:10], refs[10:]
    stored, adapter, fold, partial, shrunk, sums, line, weight, sems = refs
    depth, width = pieces[0].shape
    columns = factors[0].shape[1]
    own_rows = pl.ds(pl.multiple_of(farthest[0] * depth, depth), depth)
    tail_rows = pl.ds(pl.multiple_of(lax.rem(farthest[0], 2) * depth, depth), depth)
    lines = [pltpu.make_async_copy(v, line.at[q], sems.at[q]) for q, v in enumerate(blocks)]

    def arrive(piece, tail):
        return [
            pltpu.make_async_copy(piece, weight.at[:, pl.ds(0, width)], sems.at[2]),
            pltpu.make_async_copy(
                factors[0].at[own_rows], weight.at[:, pl.ds(width, columns)], sems.at[3]
            ),
            pltpu.make_async_copy(
                tail.at[tail_rows], weight.at[:, pl.ds(width + columns, columns)], sems.at[4]
            ),
        ]

    for copy in lines:
        copy.start()
    for number, piece in enumerate(pieces):

        @pl.when(farthest[0] == number)
        def _():
            for copy in arrive(piece, factors[1 + number // 2]):
                copy.start()

    before = pltpu.make_async_copy(total, sums, sems.at[5])
    before.start()
    for copy in lines + arrive(pieces[0], factors[1]):
        copy.wait()
    term = dot(line[0] + line[1], weight[...])
    before.wait()
    full = sums[...] + term
    partial[...] = full[:, :width].astype(partial.dtype)
    kept = jnp.where(stored[...] == adapter[...], full[:, width:], 0.0).astype(jnp.bfloat16)
    across = (((1,), (1,)), ((), ()))
    small = lax.dot_general(fold[...], kept, across, preferred_element_type=jnp.float32)
    for q in range(shrunk.shape[0]):
        shrunk[q] = small.astype(shrunk.dtype)


def own_kernel(sel, place, *refs):
    sources, refs = refs[: SOURCES - 1], refs[SOURCES - 1 :]
    halves, (base, line, weight, sems) = refs[:2], refs[2:]
    depth = sources[0].shape[1]
    steps = sel.shape[0]

    def copies(j, source, half):
        rows = pl.ds(pl.multiple_of(lax.rem(place[j], 2) * depth, depth), depth)
        return [
            pltpu.make_async_copy(source, line.at[j], sems.at[j, 0]),
            pltpu.make_async_copy(half.at[rows], weight.at[j], sems.at[j, 1]),
        ]

    for j in range(steps):
        for number, source in enumerate(sources):

            @pl.when(sel[j] == number)
            def _():
                copies(j, source, halves[0])[0].start()

        for number, half in enumerate(halves):

            @pl.when((place[j] // 2 == number) & (sel[j] < SOURCES - 1))
            def _():
                copies(j, sources[0], half)[1].start()

    for j in range(steps):

        @pl.when(sel[j] < SOURCES - 1)
        def _():
            for copy in copies(j, sources[0], halves[0]):
                copy.wait()
            term = dot(line[j], weight[j])
            if j == 0:
                base[...] = term
            else:
                base[...] += term


def last_kernel(start, farthest, everyone, stored, adapter, unfold, *refs):
    base, partial, expand, blocks, weights, refs = (
        refs[0], refs[1], refs[2:4], refs[4:6], refs[6:8], refs[8:],
    )
    out, sums, added, factor, line, weight, result, sems = refs[-8:]
    depth = weight.shape[0]
    rows = pl.ds(pl.multiple_of(farthest[0] * depth, depth), depth)
    factors = [pltpu.make_async_copy(v, factor.at[q], sems.at[q]) for q, v in enumerate(expand)]
    lines = [pltpu.make_async_copy(v, line.at[q], sems.at[2 + q]) for q, v in enumerate(blocks)]
    others = [
        pltpu.make_async_copy(base, sums, sems.at[5]),
        pltpu.make_async_copy(partial, added, sems.at[6]),
    ]
    for copy in factors + lines:
        copy.start()
    for number, half in enumerate(weights):

        @pl.when(farthest[1] == number)
        def _():
            pltpu.make_async_copy(half.at[rows], weight, sems.at[4]).start()

    for copy in others:
        copy.start()
    shrunk = jnp.sum(everyone[...].astype(jnp.float32), axis=0).astype(jnp.bfloat16)
    spread = lax.dot_general(
        shrunk, unfold[...], (((0,), (0,)), ((), ())), preferred_element_type=jnp.float32
    )
    spread = jnp.where(stored[...] == adapter[...], spread, 0.0).astype(jnp.bfloat16)
    half = spread.shape[1] // 2
    for copy in factors:
        copy.wait()
    total = dot(spread[:, :half], factor[0]) + dot(spread[:, half:], factor[1])
    for copy in lines:
        copy.wait()
    pltpu.make_async_copy(weights[0].at[rows], weight, sems.at[4]).wait()
    total += dot(line[0] + line[1], weight[...])
    for copy in others:
        copy.wait()
    result[...] = (total + sums[...] + added[...].astype(jnp.float32)).astype(result.dtype)
    copy = pltpu.make_async_copy(result, out.at[pl.ds(start, result.shape[0])], sems.at[7])
    copy.start()
    copy.wait()


def whole(shape):
    return pl.BlockSpec(shape, lambda n, *_: (0,) * len(shape))


def on_line(kernel, scalars, sources, weights, small, outs, scratch):
    rows, depth = sources[0].shape
    planes = scalars[0].shape[0]
    width = weights[0].shape[-1]
    flops = 2 * rows * planes * depth * width
    size = 2 * planes * depth * width + 2 * rows * planes * depth + 4 * rows * width
    return pl.pallas_call(
        kernel,
        grid_spec=pltpu.PrefetchScalarGridSpec(
            num_scalar_prefetch=2,
            grid=(1,),
            in_specs=[pl.BlockSpec(memory_space=pl.ANY) for _ in sources + weights]
            + [whole(v.shape) for v in small],
            out_specs=[whole(o.shape) for o in outs],
            scratch_shapes=scratch + [pltpu.SemaphoreType.DMA((planes, 4))],
        ),
        out_shape=outs,
        compiler_params=pltpu.CompilerParams(vmem_limit_bytes=VMEM_BYTES),
        cost_estimate=pl.CostEstimate(flops=flops, bytes_accessed=size, transcendentals=0),
    )(*scalars, *sources, *weights, *small)


def after(value, *events):
    return lax.optimization_barrier((value,) + events)[0]


def line_body(
    tokens, query_weight, shrink_factors, expand_factors, row_adapter_index, adapter_storage_block
):
    tp = lax.axis_size("tp")
    planes = tp // 2
    own = lax.axis_index("tp")
    z, x = own // 2, own % 2
    r, d = lax.axis_index("rep"), lax.axis_index("dp")
    rows, depth = tokens.shape
    width = query_weight.shape[1]
    holder_columns = shrink_factors.shape[1]
    holder_adapters = holder_columns // ADAPTER_RANK
    half = holder_columns // 2
    across = [(i, i ^ 1) for i in range(tp)]
    swap = [(0, 1), (1, 0)]

    def up(h):
        return [(i, i + 2) for i in range(2 * (h - 1), tp - 2)]

    def down(h):
        return [(i + 2, i) for i in range(0, tp - 2 * h)]

    def place(plane):
        return 2 * ((plane // 2) ^ d) + ((plane % 2) ^ r)

    def plane_at(p):
        return 2 * ((p // 2) ^ d) + ((p % 2) ^ r)

    pieces, starts = [], []
    first = 0
    for count in ROW_CHUNKS:
        starts.append(first)
        pieces.append(tokens[first : first + count])
        first += count
    ups = [{0: p} for p in pieces]
    downs = [{0: p} for p in pieces]

    def hop(c, h):
        ups[c][h] = lax.ppermute(ups[c][h - 1], "tp", up(h))
        downs[c][h] = lax.ppermute(downs[c][h - 1], "tp", down(h))

    def step(values, *events):
        return lax.optimization_barrier((values, events))[0]

    def to_other_core(value):
        return lax.ppermute(value, "dp", swap)

    steps = jnp.arange(planes)
    above = z + steps < planes
    hops = jnp.where(above, steps, planes - steps)
    sel = jnp.where(
        steps == 0, 0, jnp.where(hops == planes - 1, SOURCES - 1, hops + jnp.where(above, planes - 2, 0))
    ).astype(jnp.int32)
    plane = (z + steps) % planes
    places_other = place(plane).astype(jnp.int32)
    places_own = (2 * ((plane // 2) ^ d) + plane % 2).astype(jnp.int32)
    distant = jnp.where(z == 0, planes - 1, 0)
    farthest_other = place(distant).astype(jnp.int32)[None]
    farthest_own = jnp.stack([distant % 2, (distant // 2) ^ d]).astype(jnp.int32)

    blocks = query_weight.reshape(planes, depth, width)
    hop(0, 1)
    hop(1, 1)
    near = lax.ppermute(pick(blocks, 2 * r + (1 - x)), "tp", across)

    factors = shrink_factors.reshape(planes, 2, depth, holder_columns)
    leaving = jnp.concatenate([pick(pick(factors, plane_at(p)), 1 - x) for p in range(planes // 2)])
    expand_half = lax.dynamic_slice_in_dim(expand_factors, d * half, half, 0)
    expand_half = expand_half.reshape(half, tp, width).transpose(1, 0, 2)
    (ups[0][1], downs[0][1], ups[1][1], downs[1][1], near, leaving, weights, factors, expand_half) = step(
        (ups[0][1], downs[0][1], ups[1][1], downs[1][1], near, leaving, query_weight, factors, expand_half)
    )
    hop(0, 2)
    far = lax.ppermute(near, "rep", swap)
    shrink_near = lax.ppermute(leaving, "tp", across)
    near_crossed = to_other_core(near)
    pairs = weights.reshape(planes // 2, 2, depth, width)
    own_half = lax.dynamic_index_in_dim(pairs, x, 1, keepdims=False).reshape(-1, width)
    shrink_own = jnp.concatenate([pick(pick(factors, plane_at(p)), x) for p in range(planes)])
    expand_half = lax.all_to_all(expand_half, "tp", split_axis=0, concat_axis=0, tiled=True)
    expand_half = expand_half.reshape(tp * half, width)

    (ups[0][2], downs[0][2], ups[1][1], downs[1][1], shrink_near, far, near_crossed, expand_half, own_half, shrink_own, sel, places_other, places_own) = step(
        (ups[0][2], downs[0][2], ups[1][1], downs[1][1], shrink_near, far, near_crossed, expand_half, own_half, shrink_own, sel, places_other, places_own)
    )
    hop(0, 3)
    shrink = [shrink_own, shrink_near, to_other_core(shrink_near)]
    weight_other = [near, far, near_crossed, to_other_core(far)]
    weight_own = [own_half, to_other_core(own_half)]

    known = jnp.arange(adapter_storage_block.shape[0])
    stored = jnp.sum(
        jnp.where(row_adapter_index == known[None, :], adapter_storage_block[None, :], 0),
        axis=1,
        keepdims=True,
    )
    column = jnp.arange(2 * holder_columns)
    column_adapter = (own ^ (column // holder_columns)) * holder_adapters + (
        column % holder_columns
    ) // ADAPTER_RANK
    column_adapter = column_adapter[None, :].astype(jnp.int32)
    fold = (jnp.arange(ADAPTER_RANK)[:, None] == column[None, :] % ADAPTER_RANK).astype(jnp.bfloat16)
    entry = jnp.arange(tp * holder_columns)
    within = entry % (tp * half)
    entry_adapter = (within // half) * holder_adapters + (
        ((entry // (tp * half)) ^ d) * half + within % half
    ) // ADAPTER_RANK
    entry_adapter = entry_adapter[None, :].astype(jnp.int32)
    unfold = (jnp.arange(ADAPTER_RANK)[:, None] == entry[None, :] % ADAPTER_RANK).astype(jnp.bfloat16)

    def sources(c):
        between = range(1, planes - 1)
        return [pieces[c]] + [ups[c][h] for h in between] + [downs[c][h] for h in between] + [
            None
        ]

    def longest(c):
        return ups[c][planes - 1], downs[c][planes - 1]

    total_columns = width + 2 * holder_columns

    def early_part(c, *events):
        count = ROW_CHUNKS[c]
        return on_line(
            early_kernel,
            [after(sel, *events) if events else sel, places_other],
            sources(c)[:-1],
            weight_other + shrink,
            [],
            [jax.ShapeDtypeStruct((count, total_columns), jnp.float32)],
            [
                pltpu.VMEM((planes, count, depth), jnp.bfloat16),
                pltpu.VMEM((planes, depth, total_columns), jnp.bfloat16),
            ],
        )[0]

    def rest_part(c, total):
        count = ROW_CHUNKS[c]
        small = [stored[starts[c] : starts[c] + count], column_adapter, fold]
        outs = [
            jax.ShapeDtypeStruct((count, width), jnp.bfloat16),
            jax.ShapeDtypeStruct((tp, ADAPTER_RANK, count), jnp.bfloat16),
        ]
        return pl.pallas_call(
            rest_kernel,
            grid_spec=pltpu.PrefetchScalarGridSpec(
                num_scalar_prefetch=1,
                grid=(1,),
                in_specs=[pl.BlockSpec(memory_space=pl.ANY) for _ in range(10)]
                + [whole(v.shape) for v in small],
                out_specs=[whole(o.shape) for o in outs],
                scratch_shapes=[
                    pltpu.VMEM((count, total_columns), jnp.float32),
                    pltpu.VMEM((2, count, depth), jnp.bfloat16),
                    pltpu.VMEM((depth, total_columns), jnp.bfloat16),
                    pltpu.SemaphoreType.DMA((6,)),
                ],
            ),
            out_shape=outs,
            compiler_params=pltpu.CompilerParams(vmem_limit_bytes=VMEM_BYTES),
            cost_estimate=pl.CostEstimate(
                flops=2 * count * depth * total_columns, bytes_accessed=4 * depth * width, transcendentals=0
            ),
        )(farthest_other, total, *longest(c), *weight_other, *shrink, *small)

    def own_part(c, *events):
        count = ROW_CHUNKS[c]
        return on_line(
            own_kernel,
            [after(sel, *events) if events else sel, places_own],
            sources(c)[:-1],
            weight_own,
            [],
            [jax.ShapeDtypeStruct((count, width), jnp.float32)],
            [
                pltpu.VMEM((planes, count, depth), jnp.bfloat16),
                pltpu.VMEM((planes, depth, width), jnp.bfloat16),
            ],
        )[0]

    def spread_out(shrunk):
        return lax.all_to_all(shrunk, "tp", split_axis=0, concat_axis=0, tiled=True)

    def last_part(c, base, partial, everyone, expand, earlier):
        count = ROW_CHUNKS[c]
        hbm = [base, partial, *expand, *longest(c), *weight_own]
        aliases = {}
        if earlier is not None:
            aliases = {5 + len(hbm): 0}
            hbm.append(earlier)
        return pl.pallas_call(
            functools.partial(last_kernel, starts[c]),
            grid_spec=pltpu.PrefetchScalarGridSpec(
                num_scalar_prefetch=1,
                grid=(1,),
                in_specs=[
                    whole(everyone.shape),
                    whole((count, 1)),
                    whole(entry_adapter.shape),
                    whole(unfold.shape),
                ]
                + [pl.BlockSpec(memory_space=pl.ANY) for _ in hbm],
                out_specs=pl.BlockSpec(memory_space=pl.ANY),
                scratch_shapes=[
                    pltpu.VMEM((count, width), jnp.float32),
                    pltpu.VMEM((count, width), jnp.bfloat16),
                    pltpu.VMEM((2,) + expand[0].shape, jnp.bfloat16),
                    pltpu.VMEM((2, count, depth), jnp.bfloat16),
                    pltpu.VMEM((depth, width), jnp.bfloat16),
                    pltpu.VMEM((count, width), jnp.bfloat16),
                    pltpu.SemaphoreType.DMA((8,)),
                ],
            ),
            out_shape=jax.ShapeDtypeStruct((rows, width), jnp.bfloat16),
            input_output_aliases=aliases,
            compiler_params=pltpu.CompilerParams(vmem_limit_bytes=VMEM_BYTES),
            cost_estimate=pl.CostEstimate(
                flops=4 * count * width * depth, bytes_accessed=4 * depth * width, transcendentals=0
            ),
        )(
            farthest_own,
            everyone,
            stored[starts[c] : starts[c] + count],
            entry_adapter,
            unfold,
            *hbm,
        )

    early_a = early_part(0)
    base_a = own_part(0, early_a)
    (ups[0][3], ups[1][1], downs[1][1], expand_half) = step(
        (ups[0][3], ups[1][1], downs[1][1], expand_half), base_a
    )
    hop(1, 2)
    expand = [expand_half, to_other_core(expand_half)]
    partial_a, shrunk_a = rest_part(0, early_a)
    got_a = lax.ppermute(partial_a, "tp", across)
    ready = (ups[1][2], downs[1][2], farthest_own, entry_adapter, unfold)
    ready = step(ready, partial_a)
    ups[1][2], downs[1][2], farthest_own, entry_adapter, unfold = ready
    hop(1, 3)
    everyone_a = spread_out(shrunk_a)
    early_c = early_part(1)
    ups[1][3], downs[1][3] = step((ups[1][3], downs[1][3]), early_c, got_a)
    partial_c, shrunk_c = rest_part(1, early_c)
    got_c = lax.ppermute(partial_c, "tp", across)
    everyone_c = spread_out(shrunk_c)
    base_c = own_part(1, partial_c, everyone_a)
    out = last_part(0, base_a, got_a, everyone_a, expand, None)
    return last_part(1, base_c, got_c, everyone_c, expand, out)


def solution(mesh):
    placed = (
        P(("rep", "dp"), "tp"),
        P("dp", "tp"),
        P(None, ("rep", "tp")),
        P(("rep", "tp"), None),
        P(("rep", "dp"), None),
        P("rep"),
    )
    lined = dict(mesh.shape) == {"rep": 2, "tp": 8, "dp": 2}
    return jax.shard_map(
        line_body if lined else general_body,
        mesh=mesh,
        in_specs=placed,
        out_specs=P(("rep", "dp"), "tp"),
        check_vma=False,
    )
```
